768 devices in a mesh: gx: 96 (over x, z, core), gy: 8 (over y).
Axes of the slice: x: 4, y: 8, z: 12, core: 2. Of those that a mesh axis runs over, the one named last changes fastest.
Arguments:
- solution: float32 [4, 192, 10240], P(None, 'gx', 'gy'), may hold values from -0.12 to 0.12
- forcing: float32 [4, 192, 10240], P(None, 'gx', 'gy'), may hold values from -0.12 to 0.12
- viscosity: float32 [192, 10240], P('gx', 'gy'), may hold values from 0.3 to 1
- blocks: float32 [16, 192, 10240], P(None, 'gx', 'gy'), may hold values from -0.5 to 0.5, as said below
- layer_count: int32 [192, 128], P('gx', 'gy'), may hold values from 40 to 80
- bed_frozen: int32 [192, 128], P('gx', 'gy'), may hold values 0 or 1
- basin_map: int32 [192, 128], P('gx', 'gy'), may hold values from 0 to 383, as said below
Outputs:
- smoothed: float32 [4, 192, 10240], P(None, 'gx', 'gy')
- column_residual: float32 [4, 192, 128], P(None, 'gx', 'gy')
- basin_residual: float32 [4, 384], replicated
The draws below stay inside these ranges and needn't reach their ends.
Inputs may be any that keep to these rules, and one draw needn't show every extreme that they name: `blocks`: the first three diagonal entries of every cell's block are positive. `basin_map`: every basin number names some column.
All inputs are finite; a program needn't handle non-finite values. No bound on the sum of `bed_frozen` on one device may be relied on, other than what follows from the above.
Results may differ from the reference program's by a relative error of at most 0.00045.
Values sent between devices are 32-bit elements; how exact they have to be, the bound alone decides.
A program may use at most 64 MiB of HBM per device.

```python
import math
import jax
import jax.numpy as jnp
from jax import lax

CX = 2
CY = 16
LAYERS = 80
NX = 192
NY = 128
NBASIN = 384


def viscosity_field(key):
    uniform_part = jax.random.uniform(jax.random.fold_in(key, 7), (NX, NY * LAYERS), jnp.float32)
    return jnp.exp(math.log(0.3) + (0.0 - math.log(0.3)) * uniform_part)


def draw_viscosity(key, part):
    return viscosity_field(key)


def draw_blocks(key, part):
    visc_field = viscosity_field(key)
    field_shape = (NX, NY * LAYERS)
    lane_layer = jnp.arange(NY * LAYERS, dtype=jnp.int32) % LAYERS
    key_list = jax.random.split(jax.random.fold_in(key, 9), 16)
    entries = []
    for row_idx in range(4):
        for col_idx in range(4):
            uniform_part = jax.random.uniform(key_list[row_idx * 4 + col_idx], field_shape, jnp.float32)
            if row_idx < 3 and col_idx == row_idx:
                line_key = jax.random.fold_in(key, 11 + row_idx)
                weak_pick = jax.random.randint(jax.random.fold_in(line_key, 1), (NY * LAYERS,), 0, 2)
                weak_line = jnp.logical_and(weak_pick == 1, lane_layer < LAYERS // 2)
                line_base = jnp.exp(math.log(0.0001) + math.log(10.0) * jax.random.uniform(jax.random.fold_in(line_key, 2), (NY * LAYERS,), jnp.float32))
                weak_ratio = line_base[None, :] * jnp.exp(math.log(4.0) * uniform_part)
                strong_ratio = 2.0 * jnp.exp(math.log(0.003) + math.log(4.0) * uniform_part)
                entry = visc_field * jnp.where(weak_line[None, :], weak_ratio, strong_ratio)
            elif row_idx < 3 and col_idx < 3:
                entry = visc_field * (0.1 * uniform_part - 0.05)
            elif row_idx == 3 and col_idx == 3:
                entry = -(0.05 + 0.25 * uniform_part)
            else:
                entry = uniform_part - 0.5
            entries.append(entry)
    return jnp.stack(entries)


def draw_forcing(key, part):
    rough_part = 0.02 * jax.random.normal(jax.random.fold_in(key, 5), (4, NX, NY * LAYERS), jnp.float32)
    return jnp.clip(rough_part, -0.12, 0.12)


def draw_basin_map(key, part):
    shift_x = jax.random.randint(jax.random.fold_in(key, 3), (NX, NY), 0, CX)
    shift_y = jax.random.randint(jax.random.fold_in(key, 4), (NX, NY), 0, max(CY // 2, 1))
    x_pos = jnp.arange(NX, dtype=jnp.int32)[:, None]
    y_pos = jnp.arange(NY, dtype=jnp.int32)[None, :]
    across = NY // CY
    tile_x = (x_pos + shift_x) // (2 * CX) % (NX // (2 * CX))
    tile_y = (y_pos + shift_y) // CY % across
    return (tile_x * across + tile_y).astype(jnp.int32)


def with_ends(values, stream_key, low, top_value):
    longest = values.shape.index(max(values.shape))
    spots = []
    for shift in (0, 1):
        where = [jax.random.randint(jax.random.fold_in(stream_key, axis), (), 0, length) for axis, length in enumerate(values.shape)]
        where[longest] = (where[longest] + shift) % values.shape[longest]
        spots.append(tuple(where))
    return values.at[spots[0]].set(low).at[spots[1]].set(top_value)


def steps_of(own_key, extent, cuts, low, high):
    factor_of, own = 1.0, jax.random.fold_in(own_key, 6)
    for dim, shards_of in cuts:
        steps = jnp.exp(jax.random.uniform(jax.random.fold_in(own, dim), (shards_of,), jnp.float32, low / len(cuts), high / len(cuts)))
        factor_of = factor_of * jnp.repeat(steps, extent[dim] // shards_of).reshape([-1 if axis == dim else 1 for axis in range(len(extent))])
    return factor_of


def noise(rng, shape, deviation, most, cuts=(), held_as=jnp.bfloat16):
    values = jax.random.normal(rng, shape, jnp.float32) * deviation
    if len(cuts) > 0:
        values = steps_of(rng, shape, cuts, -0.22, 0.18) * values
    return jnp.clip(values, min=-most, max=most).astype(held_as)


def setup_inputs(seed: int = 0) -> dict:
    arg_keys = jax.random.split(jax.random.key(seed), 8)
    return {
        "solution": noise(arg_keys[0], (4, NX, NY * LAYERS), 0.02, 0.12, ((1, 96), (2, 8)), jnp.float32),
        "forcing": draw_forcing(jax.random.fold_in(arg_keys[7], 71), 0),
        "viscosity": draw_viscosity(jax.random.fold_in(arg_keys[7], 71), 0),
        "blocks": draw_blocks(jax.random.fold_in(arg_keys[7], 71), 0),
        "layer_count": with_ends(jax.random.randint(arg_keys[4], (NX, NY), LAYERS // 2, LAYERS + 1), jax.random.fold_in(arg_keys[4], 1), LAYERS // 2, LAYERS).astype(jnp.int32),
        "bed_frozen": with_ends((jax.random.randint(arg_keys[5], (NX, NY), 0, 2) < 1).astype(jnp.int32), jax.random.fold_in(arg_keys[5], 1), 0, 1),
        "basin_map": draw_basin_map(jax.random.fold_in(arg_keys[7], 71), 0),
    }


coupling = 0.25


def neighbour_terms(velocity, viscosity, frozen):
    grid_view = velocity.reshape(3, NX, NY, LAYERS)
    padded = jnp.pad(grid_view, ((0, 0), (1, 1), (1, 1), (0, 0)))
    lower_cells = jnp.concatenate([grid_view[..., :1] * (1.0 - frozen)[None, :, :, None], grid_view[..., :-1]], axis=-1)
    upper_cells = jnp.concatenate([grid_view[..., 1:], jnp.zeros_like(grid_view[..., :1])], axis=-1)
    along_line = 2.0 * grid_view - padded[:, :-2, 1:-1] - padded[:, 2:, 1:-1]
    across_line = padded[:, 1:-1, :-2] + padded[:, 1:-1, 2:] + lower_cells + upper_cells
    return viscosity * along_line.reshape(velocity.shape) - coupling * viscosity * across_line.reshape(velocity.shape)


def operate(masked, matrix, viscosity, frozen):
    in_cell = jnp.sum(matrix * masked[None], axis=1)
    moving = in_cell[:3] + neighbour_terms(masked[:3], viscosity, frozen)
    return jnp.concatenate([moving, in_cell[3:]], axis=0)


def line_solve(line_lead, line_off, line_rhs):
    def sweep_down(carried, cell_cols):
        gain_prev, value_prev = carried
        lead_cell, off_cell, rhs_cell = cell_cols
        pivot = lead_cell - off_cell * gain_prev
        gain = off_cell / pivot
        value = (rhs_cell + off_cell * value_prev) / pivot
        return (gain, value), (gain, value)

    zeros_line = jnp.zeros((3, line_lead.shape[2]), jnp.float32)
    scanned = (jnp.moveaxis(line_lead, 1, 0), jnp.moveaxis(line_off, 1, 0), jnp.moveaxis(line_rhs, 1, 0))
    _, (gains, values) = lax.scan(sweep_down, (zeros_line, zeros_line), scanned)

    def sweep_up(next_value, cell_cols):
        gain, value = cell_cols
        solved = value + gain * next_value
        return solved, solved

    _, corrections = lax.scan(sweep_up, zeros_line, (gains, values), reverse=True)
    return jnp.moveaxis(corrections, 0, 1)


def reference(solution, forcing, viscosity, blocks, layer_count, bed_frozen, basin_map):
    layer_idx = jnp.arange(LAYERS, dtype=jnp.int32)
    active = (layer_idx[None, None, :] < layer_count[:, :, None]).astype(jnp.float32).reshape(NX, NY * LAYERS)
    frozen = bed_frozen.astype(jnp.float32)
    matrix = blocks.reshape(4, 4, NX, NY * LAYERS)
    masked = solution * active[None]
    residual = active[None] * (forcing - operate(masked, matrix, viscosity, frozen))
    diagonal = jnp.stack([matrix[0, 0], matrix[1, 1], matrix[2, 2]])
    line_lead = jnp.where(active[None] > 0.0, diagonal + 2.0 * viscosity[None], 1.0)
    line_off = jnp.broadcast_to((viscosity * active)[None], line_lead.shape)
    correction = line_solve(line_lead, line_off, residual[:3])
    pressure_in = residual[3] - (matrix[3, 0] * correction[0] + matrix[3, 1] * correction[1] + matrix[3, 2] * correction[2])
    pressure_step = active * pressure_in / viscosity
    smoothed = solution + jnp.concatenate([correction, pressure_step[None]], axis=0)
    post = active[None] * (forcing - operate(smoothed * active[None], matrix, viscosity, frozen))
    column_residual = jnp.sum(post.reshape(4, NX, NY, LAYERS), axis=-1)
    basin_residual = jax.ops.segment_sum(column_residual.reshape(4, NX * NY).T, basin_map.reshape(-1), num_segments=NBASIN).T
    return smoothed, column_residual, basin_residual
```

```python
import functools

import jax
import jax.numpy as jnp
from jax import lax
from jax.experimental import pallas as pl
from jax.experimental.pallas import tpu as pltpu
from jax.sharding import PartitionSpec as P

MESH = pl.DeviceIdType.MESH
HIGHEST = lax.Precision.HIGHEST
F32 = jnp.float32
LANE = 128


def factors(count_x):
    return (4, count_x // 8) if count_x == 96 else (2, count_x // 4)


def roll(value, shift, axis=1):
    size = value.shape[axis]
    return pltpu.roll(value, shift % size, axis)


def eliminate_levels(count):
    left = list(range(count))
    levels = []
    while len(left) > 1:
        gone = [pos for pos in range(0, len(left) - 1, 2)]
        levels.append([(left[p], left[p - 1] if p else None, left[p + 1]) for p in gone])
        left = [cell for pos, cell in enumerate(left) if pos not in gone]
    return levels


def solve_lines(load, store, count):
    sub = lax.broadcasted_iota(jnp.int32, (8, LANE), 0)
    first = sub == 0
    d0, d1, r0, r1 = ([load(t, q) for t in range(count)] for q in range(4))
    on0 = [d >= 0.0 for d in d0]
    on1 = [d >= 0.0 for d in d1]
    one, zero = jnp.full((8, LANE), 1.0, F32), jnp.zeros((8, LANE), F32)
    flag1 = [jnp.where(on, one, zero) for on in on1]
    before = [jnp.where(first, zero, roll(flag1[-1], 1, 0))] + flag1[:-1]
    edge_in = [jnp.where(on, b, zero) for on, b in zip(on0, before)]
    edge_mid = [jnp.where(on, f, zero) for on, f in zip(on0, flag1)]
    edge_out = edge_in[1:] + [roll(edge_in[0], -1, 0)]
    leak0 = [jnp.where(on, d + (2.0 - a - b), one) for on, d, a, b in zip(on0, d0, edge_in, edge_mid)]
    leak1 = [jnp.where(on, d + (2.0 - a - b), one) for on, d, a, b in zip(on1, d1, edge_mid, edge_out)]
    inv0 = [1.0 / (d + (a + b)) for d, a, b in zip(leak0, edge_in, edge_mid)]
    part_leak = [d * i for d, i in zip(leak0, inv0)]
    part_src = [r * i for r, i in zip(r0, inv0)]
    give_leak = [e * p for e, p in zip(edge_in, part_leak)]
    give_src = [e * p for e, p in zip(edge_in, part_src)]
    give_leak = give_leak[1:] + [roll(give_leak[0], -1, 0)]
    give_src = give_src[1:] + [roll(give_src[0], -1, 0)]
    leak = [d + (e * p + g) for d, e, p, g in zip(leak1, edge_mid, part_leak, give_leak)]
    src = [r + (e * p + g) for r, e, p, g in zip(r1, edge_mid, part_src, give_src)]
    edge = [a * (b * i) for a, b, i in zip(edge_in, edge_mid, inv0)]
    kept = {}
    for level in eliminate_levels(count):
        updates = []
        for cell, low, high in level:
            lo_edge, hi_edge = edge[cell], edge[high]
            inv = 1.0 / (leak[cell] + (lo_edge + hi_edge))
            lo_share, hi_share = lo_edge * inv, hi_edge * inv
            kept[cell] = (lo_share, hi_share, src[cell] * inv)
            updates.append((cell, low, high, lo_edge * hi_share, lo_share, hi_share))
        for cell, low, high, joined, lo_share, hi_share in updates:
            lo_leak, lo_src = lo_share * leak[cell], lo_share * src[cell]
            if low is None:
                low, lo_leak, lo_src = count - 1, roll(lo_leak, -1, 0), roll(lo_src, -1, 0)
            leak[low], src[low] = leak[low] + lo_leak, src[low] + lo_src
            leak[high], src[high] = leak[high] + hi_share * leak[cell], src[high] + hi_share * src[cell]
            edge[high] = joined
    last_leak, last_src, lo_edge = leak[-1], src[-1], edge[-1]
    hi_edge = roll(lo_edge, -1, 0)
    for hop in (1, 2, 4):
        inv = 1.0 / (last_leak + (lo_edge + hi_edge))
        p_leak, p_src, p_lo, p_hi = last_leak * inv, last_src * inv, lo_edge * inv, hi_edge * inv
        last_leak = last_leak + (lo_edge * roll(p_leak, hop, 0) + hi_edge * roll(p_leak, -hop, 0))
        last_src = last_src + (lo_edge * roll(p_src, hop, 0) + hi_edge * roll(p_src, -hop, 0))
        lo_edge, hi_edge = lo_edge * roll(p_lo, hop, 0), hi_edge * roll(p_hi, -hop, 0)
    value = [None] * count
    value[-1] = last_src / last_leak
    wrapped = roll(value[-1], 1, 0)
    for level in reversed(eliminate_levels(count)):
        for cell, low, high in level:
            lo_share, hi_share, own = kept[cell]
            lower = wrapped if low is None else value[low]
            value[cell] = own + (lo_share * lower + hi_share * value[high])
    for t in range(count):
        lower = wrapped if t == 0 else value[t - 1]
        store(t, 0, part_src[t] + (edge_in[t] * lower + edge_mid[t] * value[t]) * inv0[t])
        store(t, 1, value[t])


def sweep_kernel(
    count_x, count_y, basins,
    sol_ref, forc_ref, visc_ref, blk_ref, layers_ref, frozen_ref, basin_ref,
    smooth_ref, column_ref, total_ref,
    halo_out, halo_in, row_out, row_in, line_out, line_in,
    core_out, core_in, ring_buf, plane_buf, send_sem, recv_sem,
):
    cx, cz = factors(count_x)
    rows, lanes = visc_ref.shape
    y_cells = layers_ref.shape[1]
    layers = lanes // y_cells
    chunks = lanes // LANE
    owners = 3 * chunks
    seg = count_x // 8
    gx, gy = lax.axis_index("gx"), lax.axis_index("gy")
    core = lax.rem(gx, 2)
    pz = lax.rem(lax.div(gx, 2), cz)
    px = lax.div(gx, 2 * cz)
    partner = gx + 1 - 2 * core
    up_y = lax.rem(gy + 1, count_y)
    down_y = lax.rem(gy + count_y - 1, count_y)

    def plane_peer(i):
        x = lax.rem(px + lax.div(i, count_y), cx)
        y = lax.rem(gy + lax.rem(i, count_y), count_y)
        return x, y

    def gx_of(x, z, c):
        return (x * cz + z) * 2 + c

    barrier = pltpu.get_barrier_semaphore()

    def greet_line(i, carry):
        pl.semaphore_signal(barrier, inc=1, device_id=(lax.rem(gx + i, count_x), gy), device_id_type=MESH)
        return carry

    def greet_plane(i, carry):
        x = lax.rem(px + lax.div(i, count_y - 1), cx)
        y = lax.rem(gy + 1 + lax.rem(i, count_y - 1), count_y)
        pl.semaphore_signal(barrier, inc=1, device_id=(gx_of(x, pz, core), y), device_id_type=MESH)
        return carry

    lax.fori_loop(1, count_x, greet_line, 0)
    lax.fori_loop(0, cx * (count_y - 1), greet_plane, 0)

    def remote(src, dst, k, to):
        return pltpu.make_async_remote_copy(
            src_ref=src, dst_ref=dst, send_sem=send_sem.at[k], recv_sem=recv_sem.at[k],
            device_id=to, device_id_type=MESH,
        )

    def wait_rows(sem, ref, count):
        view = ref.at[pl.ds(0, count)]
        pltpu.make_async_copy(view, view, sem).wait()

    lane = lax.broadcasted_iota(jnp.int32, (rows, lanes), 1)

    def cell_of(index):
        return ((index.astype(F32) + 0.5) * (1.0 / layers)).astype(jnp.int32)

    layer = lane - cell_of(lane) * layers
    wide = lax.broadcasted_iota(jnp.int32, (y_cells, lanes), 1)
    spread = jnp.where(
        cell_of(wide) == lax.broadcasted_iota(jnp.int32, (y_cells, lanes), 0), 1.0, 0.0
    ).astype(F32)
    filled = jnp.dot(layers_ref[...].astype(F32), spread, precision=HIGHEST, preferred_element_type=F32)
    frozen = jnp.dot(frozen_ref[...].astype(F32), spread, precision=HIGHEST, preferred_element_type=F32)
    active = layer.astype(F32) + 0.5 < filled
    bottom, top = layer == 0, layer == layers - 1
    slide = 1.0 - frozen

    def masked(value):
        return jnp.where(active, value, 0.0)

    state = [masked(sol_ref[k]) for k in range(4)]
    small = lax.broadcasted_iota(jnp.int32, (rows, LANE), 1)

    def send_halo(values, k):
        for c in range(3):
            upward = jnp.where(small < layers, roll(values[c][:, lanes - LANE:], layers), 0.0)
            downward = jnp.where(small >= LANE - layers, roll(values[c][:, :LANE], LANE - layers), 0.0)
            halo_out[k, 0, pl.ds(c * rows, rows)] = upward
            halo_out[k, 1, pl.ds(c * rows, rows)] = downward
        up = remote(halo_out.at[k, 0], halo_in.at[k, 0], k * 2, (gx, up_y))
        down = remote(halo_out.at[k, 1], halo_in.at[k, 1], k * 2 + 1, (gx, down_y))
        up.start()
        down.start()
        return up, down

    def neighbours(values, k):
        out = []
        for c in range(3):
            v = values[c]
            low = jnp.where(gy > 0, halo_in[k, 0, pl.ds(c * rows, rows)], 0.0)
            high = jnp.where(gy < count_y - 1, halo_in[k, 1, pl.ds(c * rows, rows)], 0.0)
            before = jnp.where(lane < layers, 0.0, roll(v, layers))
            after = jnp.where(lane >= lanes - layers, 0.0, roll(v, lanes - layers))
            below = jnp.where(bottom, v * slide, roll(v, 1))
            above = jnp.where(top, 0.0, roll(v, lanes - 1))
            total = (before + after) + (below + above)
            if chunks > 1:
                pad = jnp.zeros((rows, lanes - LANE), F32)
                total = total + (jnp.concatenate([low, pad], 1) + jnp.concatenate([pad, high], 1))
            else:
                total = total + (low + high)
            out.append(total)
        return out

    def block(k, j):
        return blk_ref[4 * k + j]

    inv_visc = 1.0 / visc_ref[...]
    diag = [jnp.where(active, block(k, k) * inv_visc, -1.0) for k in range(3)]
    rest = []
    for k in range(3):
        acc = forc_ref[k]
        for j in range(4):
            if j != k:
                acc = acc - block(k, j) * state[j]
        rest.append(acc * inv_visc)

    pl.semaphore_wait(barrier, count_x - 1 + cx * (count_y - 1))
    first_halo = send_halo(state[:3], 0)
    for copy in first_halo:
        copy.wait_recv()
    around = neighbours(state[:3], 0)
    for k in range(3):
        rhs = masked(rest[k] + 0.25 * around[k])
        for j in range(chunks):
            at = (k * chunks + j) * 2 * rows
            row_out[pl.ds(at, rows)] = diag[k][:, j * LANE:(j + 1) * LANE]
            row_out[pl.ds(at + rows, rows)] = rhs[:, j * LANE:(j + 1) * LANE]

    wide_rows = 2 * rows

    def owner_of(q):
        return lax.div(q * count_x, owners)

    def to_owner(q, carry):
        to = owner_of(q)
        src = row_out.at[pl.ds(pl.multiple_of(q * wide_rows, wide_rows), wide_rows)]
        dst = row_in.at[pl.ds(pl.multiple_of(gx * wide_rows, wide_rows), wide_rows)]

        @pl.when(to == gx)
        def _():
            pltpu.make_async_copy(src, dst, recv_sem.at[4]).start()

        @pl.when(to != gx)
        def _():
            remote(src, dst, 4, (to, gy)).start()

        return carry

    lax.fori_loop(0, owners, to_owner, 0)
    mine = lax.div(owners * gx + count_x - 1, count_x)
    owning = jnp.logical_and(mine < owners, owner_of(mine) == gx)

    @pl.when(owning)
    def _():
        wait_rows(recv_sem.at[4], row_in, count_x * wide_rows)

        def load(t, q):
            return row_in[pl.ds(t * wide_rows + q, 8, stride=seg * wide_rows), :]

        def store(t, r, value):
            line_out[pl.ds(t * rows + r, 8, stride=seg * rows), :] = value

        solve_lines(load, store, seg)

        def give(i, carry):
            to = lax.rem(gx + i, count_x)
            src = line_out.at[pl.ds(pl.multiple_of(to * rows, rows), rows)]
            dst = line_in.at[pl.ds(pl.multiple_of(mine * rows, rows), rows)]

            @pl.when(i == count_x)
            def _():
                pltpu.make_async_copy(src, dst, recv_sem.at[5]).start()

            @pl.when(i != count_x)
            def _():
                remote(src, dst, 5, (to, gy)).start()

            return carry

        lax.fori_loop(1, count_x + 1, give, 0)

    eye = lax.broadcasted_iota(jnp.int32, (y_cells, y_cells), 0) == lax.broadcasted_iota(
        jnp.int32, (y_cells, y_cells), 1
    )
    names = basin_ref[...].astype(F32)
    wide_basins = basins
    basin_idx = lax.broadcasted_iota(jnp.int32, (y_cells, wide_basins), 1).astype(F32)
    member = []
    for x in range(rows):
        column = jnp.sum(jnp.where(eye, names[x:x + 1], 0.0), axis=1, keepdims=True)
        member.append(jnp.where(basin_idx == column, 1.0, 0.0).astype(F32))

    wait_rows(recv_sem.at[5], line_in, owners * rows)
    solved = [
        jnp.concatenate([line_in[pl.ds((k * chunks + j) * rows, rows)] for j in range(chunks)], 1)
        for k in range(3)
    ]
    change = [solved[k] - state[k] for k in range(3)]
    second_halo = send_halo(change, 1)
    acc = forc_ref[3] - block(3, 3) * state[3]
    for k in range(3):
        acc = acc - block(3, k) * solved[k]
    step = masked(acc * inv_visc)
    for k in range(3):
        smooth_ref[k] = jnp.where(active, solved[k], sol_ref[k])
    smooth_ref[3] = sol_ref[3] + step
    post = []
    for k in range(3):
        acc = block(k, 3) * step
        for j in range(3):
            if j != k:
                acc = acc + block(k, j) * change[j]
        post.append(acc)
    for copy in second_halo:
        copy.wait_recv()
    around = neighbours(change, 1)
    post = [masked(0.25 * visc_ref[...] * around[k] - post[k]) for k in range(3)]
    post.append((visc_ref[...] - block(3, 3)) * step)
    by_row = jnp.concatenate([post[k][x:x + 1] for x in range(rows) for k in range(4)], 0)
    sums = lax.dot_general(
        by_row, spread, (((1,), (1,)), ((), ())), precision=HIGHEST, preferred_element_type=F32
    )
    for x in range(rows):
        for k in range(4):
            column_ref[k, x:x + 1, :] = sums[4 * x + k:4 * x + k + 1]
    part = jnp.dot(sums[0:4], member[0], precision=HIGHEST, preferred_element_type=F32)
    for x in range(1, rows):
        part = part + jnp.dot(
            sums[4 * x:4 * x + 4], member[x], precision=HIGHEST, preferred_element_type=F32
        )

    pieces = wide_basins // LANE
    size = 2 * pieces

    def packed(pair):
        return jnp.concatenate([pair[:, j * LANE:(j + 1) * LANE] for j in range(pieces)], 0)

    lower, upper = packed(part[0:2]), packed(part[2:4])
    core_out[0] = jnp.where(core == 0, upper, lower)
    first = remote(core_out.at[0], core_in.at[0], 6, (partner, gy))
    first.start()
    first.wait_recv()
    own = jnp.where(core == 0, lower, upper) + core_in[0]
    ring_buf[pz] = own

    def to_ring(i, carry):
        z = lax.rem(pz + i, cz)
        remote(ring_buf.at[pz], ring_buf.at[pz], 7, (gx_of(px, z, core), gy)).start()
        return carry

    lax.fori_loop(1, cz, to_ring, 0)
    wait_rows(recv_sem.at[7], ring_buf, cz - 1)
    own = ring_buf[0]
    for i in range(1, cz):
        own = own + ring_buf[i]
    here = px * count_y + gy
    plane_buf[here] = own

    def to_plane(i, carry):
        x, y = plane_peer(i)
        remote(plane_buf.at[here], plane_buf.at[here], 8, (gx_of(x, pz, core), y)).start()
        return carry

    lax.fori_loop(1, cx * count_y, to_plane, 0)
    wait_rows(recv_sem.at[8], plane_buf, cx * count_y - 1)
    own = plane_buf[0]
    for i in range(1, cx * count_y):
        own = own + plane_buf[i]
    core_out[1] = own
    last = remote(core_out.at[1], core_in.at[1], 9, (partner, gy))
    last.start()
    last.wait_recv()
    other = core_in[1]
    lower, upper = jnp.where(core == 0, own, other), jnp.where(core == 0, other, own)
    for j in range(pieces):
        width = min(LANE, total_ref.shape[1] - j * LANE)
        if width > 0:
            total_ref[0:2, j * LANE:j * LANE + width] = lower[2 * j:2 * j + 2, :width]
            total_ref[2:4, j * LANE:j * LANE + width] = upper[2 * j:2 * j + 2, :width]

    for copy in first_halo + second_halo + (first, last):
        copy.wait_send()

    @pl.when(owning)
    def _():
        wait_rows(send_sem.at[4], row_out, (owners - 1) * wide_rows)
        wait_rows(send_sem.at[5], line_out, (count_x - 1) * rows)

    @pl.when(jnp.logical_not(owning))
    def _():
        wait_rows(send_sem.at[4], row_out, owners * wide_rows)

    wait_rows(send_sem.at[7], ring_buf, cz - 1)
    wait_rows(send_sem.at[8], plane_buf, cx * count_y - 1)


def solution(mesh):
    count_x, count_y = mesh.shape["gx"], mesh.shape["gy"]
    cx, cz = factors(count_x)

    def local(sol, forc, visc, blocks, layers, frozen, basin_map):
        rows, lanes = visc.shape
        chunks = lanes // LANE
        owners = 3 * chunks
        basins = count_x // 2 * count_y
        padded = -(-basins // LANE) * LANE
        size = 2 * padded // LANE
        vmem = pl.BlockSpec(memory_space=pltpu.VMEM)
        return pl.pallas_call(
            functools.partial(sweep_kernel, count_x, count_y, padded),
            out_shape=(
                jax.ShapeDtypeStruct(sol.shape, F32),
                jax.ShapeDtypeStruct((4,) + layers.shape, F32),
                jax.ShapeDtypeStruct((4, basins), F32),
            ),
            in_specs=[vmem] * 7,
            out_specs=(vmem, vmem, vmem),
            scratch_shapes=[
                pltpu.VMEM((2, 2, 8, LANE), F32),
                pltpu.VMEM((2, 2, 8, LANE), F32),
                pltpu.VMEM((owners * 2 * rows, LANE), F32),
                pltpu.VMEM((count_x * 2 * rows, LANE), F32),
                pltpu.VMEM((count_x * rows, LANE), F32),
                pltpu.VMEM((owners * rows, LANE), F32),
                pltpu.VMEM((2, size, LANE), F32),
                pltpu.VMEM((2, size, LANE), F32),
                pltpu.VMEM((cz, size, LANE), F32),
                pltpu.VMEM((cx * count_y, size, LANE), F32),
                pltpu.SemaphoreType.DMA((10,)),
                pltpu.SemaphoreType.DMA((10,)),
            ],
            compiler_params=pltpu.CompilerParams(
                collective_id=0, has_side_effects=True, vmem_limit_bytes=32 * 2**20
            ),
            name="sweep",
        )(sol, forc, visc, blocks, layers, frozen, basin_map)

    return jax.shard_map(
        local,
        mesh=mesh,
        in_specs=(
            P(None, "gx", "gy"), P(None, "gx", "gy"), P("gx", "gy"), P(None, "gx", "gy"),
            P("gx", "gy"), P("gx", "gy"), P("gx", "gy"),
        ),
        out_specs=(P(None, "gx", "gy"), P(None, "gx", "gy"), P()),
        check_vma=False,
    )
```

```python
import functools

import jax
import jax.numpy as jnp
from jax import lax
from jax.experimental import pallas as pl
from jax.experimental.pallas import tpu as pltpu
from jax.sharding import PartitionSpec as P

MESH = pl.DeviceIdType.MESH
HIGHEST = lax.Precision.HIGHEST
F32 = jnp.float32
LANE = 128


def factors(count_x):
    return (4, count_x // 8) if count_x == 96 else (2, count_x // 4)


def roll(value, shift, axis=1):
    size = value.shape[axis]
    return pltpu.roll(value, shift % size, axis)


def eliminate_levels(count):
    left = list(range(count))
    levels = []
    while len(left) > 1:
        gone = [pos for pos in range(0, len(left) - 1, 2)]
        levels.append([(left[p], left[p - 1] if p else None, left[p + 1]) for p in gone])
        left = [cell for pos, cell in enumerate(left) if pos not in gone]
    return levels


def solve_lines(load, store, count):
    sub = lax.broadcasted_iota(jnp.int32, (8, LANE), 0)
    first = sub == 0
    d0, d1, r0, r1 = ([load(t, q) for t in range(count)] for q in range(4))
    on0 = [d >= 0.0 for d in d0]
    on1 = [d >= 0.0 for d in d1]
    one, zero = jnp.full((8, LANE), 1.0, F32), jnp.zeros((8, LANE), F32)
    r0 = [jnp.where(on, r, zero) for on, r in zip(on0, r0)]
    r1 = [jnp.where(on, r, zero) for on, r in zip(on1, r1)]
    flag1 = [jnp.where(on, one, zero) for on in on1]
    before = [jnp.where(first, zero, roll(flag1[-1], 1, 0))] + flag1[:-1]
    edge_in = [jnp.where(on, b, zero) for on, b in zip(on0, before)]
    edge_mid = [jnp.where(on, f, zero) for on, f in zip(on0, flag1)]
    edge_out = edge_in[1:] + [roll(edge_in[0], -1, 0)]
    leak0 = [jnp.where(on, d + (2.0 - a - b), one) for on, d, a, b in zip(on0, d0, edge_in, edge_mid)]
    leak1 = [jnp.where(on, d + (2.0 - a - b), one) for on, d, a, b in zip(on1, d1, edge_mid, edge_out)]
    inv0 = [1.0 / (d + (a + b)) for d, a, b in zip(leak0, edge_in, edge_mid)]
    part_leak = [d * i for d, i in zip(leak0, inv0)]
    part_src = [r * i for r, i in zip(r0, inv0)]
    give_leak = [e * p for e, p in zip(edge_in, part_leak)]
    give_src = [e * p for e, p in zip(edge_in, part_src)]
    give_leak = give_leak[1:] + [roll(give_leak[0], -1, 0)]
    give_src = give_src[1:] + [roll(give_src[0], -1, 0)]
    leak = [d + (e * p + g) for d, e, p, g in zip(leak1, edge_mid, part_leak, give_leak)]
    src = [r + (e * p + g) for r, e, p, g in zip(r1, edge_mid, part_src, give_src)]
    edge = [a * (b * i) for a, b, i in zip(edge_in, edge_mid, inv0)]
    kept = {}
    for level in eliminate_levels(count):
        updates = []
        for cell, low, high in level:
            lo_edge, hi_edge = edge[cell], edge[high]
            inv = 1.0 / (leak[cell] + (lo_edge + hi_edge))
            lo_share, hi_share = lo_edge * inv, hi_edge * inv
            kept[cell] = (lo_share, hi_share, src[cell] * inv)
            updates.append((cell, low, high, lo_edge * hi_share, lo_share, hi_share))
        for cell, low, high, joined, lo_share, hi_share in updates:
            lo_leak, lo_src = lo_share * leak[cell], lo_share * src[cell]
            if low is None:
                low, lo_leak, lo_src = count - 1, roll(lo_leak, -1, 0), roll(lo_src, -1, 0)
            leak[low], src[low] = leak[low] + lo_leak, src[low] + lo_src
            leak[high], src[high] = leak[high] + hi_share * leak[cell], src[high] + hi_share * src[cell]
            edge[high] = joined
    last_leak, last_src, lo_edge = leak[-1], src[-1], edge[-1]
    hi_edge = roll(lo_edge, -1, 0)
    for hop in (1, 2, 4):
        inv = 1.0 / (last_leak + (lo_edge + hi_edge))
        p_leak, p_src, p_lo, p_hi = last_leak * inv, last_src * inv, lo_edge * inv, hi_edge * inv
        last_leak = last_leak + (lo_edge * roll(p_leak, hop, 0) + hi_edge * roll(p_leak, -hop, 0))
        last_src = last_src + (lo_edge * roll(p_src, hop, 0) + hi_edge * roll(p_src, -hop, 0))
        lo_edge, hi_edge = lo_edge * roll(p_lo, hop, 0), hi_edge * roll(p_hi, -hop, 0)
    value = [None] * count
    value[-1] = last_src / last_leak
    wrapped = roll(value[-1], 1, 0)
    for level in reversed(eliminate_levels(count)):
        for cell, low, high in level:
            lo_share, hi_share, own = kept[cell]
            lower = wrapped if low is None else value[low]
            value[cell] = own + (lo_share * lower + hi_share * value[high])
    for t in range(count):
        lower = wrapped if t == 0 else value[t - 1]
        store(t, 0, part_src[t] + (edge_in[t] * lower + edge_mid[t] * value[t]) * inv0[t])
        store(t, 1, value[t])


def far_first(i, count):
    side = 1 - 2 * lax.rem(i, 2)
    return count // 2 + side * lax.div(i + 1, 2)


def sweep_kernel(
    count_x, count_y, basins,
    sol_hbm, forc_hbm, visc_hbm, blk_hbm, layers_hbm, frozen_hbm, basin_hbm,
    smooth_ref, column_ref, total_ref,
    sol_ref, forc_ref, visc_ref, blk_ref, layers_ref, frozen_ref, basin_ref,
    edge_out, edge_in, halo_out, halo_in, row_out, row_in, line_out, line_in,
    core_out, core_in, ring_buf, plane_buf, load_sem, send_sem, recv_sem, ready_sem,
):
    cx, cz = factors(count_x)
    rows, lanes = visc_ref.shape
    y_cells = layers_ref.shape[1]
    layers = lanes // y_cells
    chunks = lanes // LANE
    owners = 3 * chunks
    seg = count_x // 8
    z_step = 2 if cz >= 8 else 1
    z_owning = -(-owners // (2 * cx))
    gx, gy = lax.axis_index("gx"), lax.axis_index("gy")
    core = lax.rem(gx, 2)
    pz = lax.rem(lax.div(gx, 2), cz)
    px = lax.div(gx, 2 * cz)
    partner = gx + 1 - 2 * core
    mine = (lax.div(pz, z_step) * cx + px) * 2 + core
    owning = jnp.logical_and(lax.rem(pz, z_step) == 0, mine < owners)
    my_chunk = lax.rem(mine, chunks)
    low_edge = jnp.logical_and(owning, my_chunk == 0)
    high_edge = jnp.logical_and(owning, my_chunk == chunks - 1)

    def along_y(step):
        return lax.rem(gy + step + count_y, count_y)

    def gx_of(x, z, c):
        return (x * cz + z) * 2 + c

    def owner_of(q):
        return gx_of(lax.rem(lax.div(q, 2), cx), lax.div(q, 2 * cx) * z_step, lax.rem(q, 2))

    loads = [
        pltpu.make_async_copy(src, dst, load_sem.at[i])
        for i, (src, dst) in enumerate((
            (layers_hbm, layers_ref), (frozen_hbm, frozen_ref), (sol_hbm, sol_ref),
            (visc_hbm, visc_ref), (blk_hbm, blk_ref), (forc_hbm, forc_ref), (basin_hbm, basin_ref),
        ))
    ]
    for copy in loads:
        copy.start()

    barrier = pltpu.get_barrier_semaphore()

    def greet(y):
        def one(i, carry):
            pl.semaphore_signal(
                barrier, inc=1, device_id=(lax.rem(gx + i, count_x), y), device_id_type=MESH
            )
            return carry

        return one

    @pl.when(owning)
    def _():
        lax.fori_loop(1, count_x, greet(gy), 0)

    @pl.when(low_edge)
    def _():
        lax.fori_loop(0, count_x, greet(along_y(-1)), 0)

    @pl.when(high_edge)
    def _():
        lax.fori_loop(0, count_x, greet(along_y(1)), 0)

    def remote(src, dst, k, to):
        return pltpu.make_async_remote_copy(
            src_ref=src, dst_ref=dst, send_sem=send_sem.at[k], recv_sem=recv_sem.at[k],
            device_id=to, device_id_type=MESH,
        )

    def wait_rows(sem, ref, count):
        view = ref.at[pl.ds(0, count)]
        pltpu.make_async_copy(view, view, sem).wait()

    lane = lax.broadcasted_iota(jnp.int32, (rows, lanes), 1)

    def cell_of(index):
        return ((index.astype(F32) + 0.5) * (1.0 / layers)).astype(jnp.int32)

    layer = lane - cell_of(lane) * layers
    wide = lax.broadcasted_iota(jnp.int32, (y_cells, lanes), 1)
    spread = jnp.where(
        cell_of(wide) == lax.broadcasted_iota(jnp.int32, (y_cells, lanes), 0), 1.0, 0.0
    ).astype(F32)
    loads[0].wait()
    loads[1].wait()
    filled = jnp.dot(layers_ref[...].astype(F32), spread, precision=HIGHEST, preferred_element_type=F32)
    frozen = jnp.dot(frozen_ref[...].astype(F32), spread, precision=HIGHEST, preferred_element_type=F32)
    active = layer.astype(F32) + 0.5 < filled
    bottom, top = layer == 0, layer == layers - 1
    slide = 1.0 - frozen

    def masked(value):
        return jnp.where(active, value, 0.0)

    loads[2].wait()
    state = [masked(sol_ref[k]) for k in range(4)]
    small = lax.broadcasted_iota(jnp.int32, (rows, LANE), 1)

    def facing_up(value):
        return jnp.where(small < layers, roll(value[:, lanes - LANE:], layers), 0.0)

    def facing_down(value):
        return jnp.where(small >= LANE - layers, roll(value[:, :LANE], LANE - layers), 0.0)

    def inner_neighbours(values):
        out = []
        for v in values:
            before = jnp.where(lane < layers, 0.0, roll(v, layers))
            after = jnp.where(lane >= lanes - layers, 0.0, roll(v, lanes - layers))
            below = jnp.where(bottom, v * slide, roll(v, 1))
            above = jnp.where(top, 0.0, roll(v, lanes - 1))
            out.append((before + after) + (below + above))
        return out

    def block(k, j):
        return blk_ref[4 * k + j]

    for k in range(3):
        edge_out[pl.ds((2 * k) * rows, rows)] = facing_up(state[k])
        edge_out[pl.ds((2 * k + 1) * rows, rows)] = facing_down(state[k])
    around = inner_neighbours(state[:3])
    wide_rows = 2 * rows
    loads[3].wait()
    loads[4].wait()
    loads[5].wait()
    inv_visc = 1.0 / visc_ref[...]
    for k in range(3):
        acc = forc_ref[k]
        for j in range(4):
            if j != k:
                acc = acc - block(k, j) * state[j]
        rhs = masked(acc * inv_visc + 0.25 * around[k])
        diag = jnp.where(active, block(k, k) * inv_visc, -1.0)
        for j in range(chunks):
            at = (k * chunks + j) * wide_rows
            row_out[pl.ds(at, rows)] = diag[:, j * LANE:(j + 1) * LANE]
            row_out[pl.ds(at + rows, rows)] = rhs[:, j * LANE:(j + 1) * LANE]

    @pl.when(owning)
    def _():
        pl.semaphore_wait(barrier, owners + 6 - 1)

    @pl.when(jnp.logical_not(owning))
    def _():
        pl.semaphore_wait(barrier, owners + 6)

    for k in range(3):
        for side, step, chunk in ((0, 1, 0), (1, -1, chunks - 1)):
            remote(
                edge_out.at[pl.ds((2 * k + side) * rows, rows)],
                edge_in.at[side, pl.ds(pl.multiple_of(gx * rows, rows), rows)],
                side, (owner_of(k * chunks + chunk), along_y(step)),
            ).start()

    def to_owner(i, carry):
        x = lax.rem(px + far_first(lax.rem(lax.div(i, 2), cx), cx), cx)
        q = ((z_owning - 1 - lax.div(i, 2 * cx)) * cx + x) * 2 + lax.rem(i, 2)
        to = owner_of(q)
        at = jnp.minimum(q, owners - 1)
        src = row_out.at[pl.ds(pl.multiple_of(at * wide_rows, wide_rows), wide_rows)]
        dst = row_in.at[pl.ds(pl.multiple_of(gx * wide_rows, wide_rows), wide_rows)]

        @pl.when(to == gx)
        def _():
            @pl.when(q < owners)
            def _():
                pltpu.make_async_copy(src, dst, recv_sem.at[4]).start()

        @pl.when(jnp.logical_and(to != gx, q < owners))
        def _():
            remote(src, dst, 4, (to, gy)).start()

        return carry

    lax.fori_loop(0, 2 * cx * z_owning, to_owner, 0)

    @pl.when(owning)
    def _():
        @pl.when(low_edge)
        def _():
            wait_rows(recv_sem.at[0], edge_in.at[0], count_x * rows)

        @pl.when(high_edge)
        def _():
            wait_rows(recv_sem.at[1], edge_in.at[1], count_x * rows)

        wait_rows(recv_sem.at[4], row_in, count_x * wide_rows)
        low_on = jnp.logical_and(my_chunk == 0, gy > 0)
        high_on = jnp.logical_and(my_chunk == chunks - 1, gy < count_y - 1)

        def load(t, q):
            value = row_in[pl.ds(t * wide_rows + q, 8, stride=seg * wide_rows), :]
            if q >= rows:
                at = pl.ds(t * rows + q - rows, 8, stride=seg * rows)
                low = jnp.where(low_on, edge_in[0, at, :], 0.0)
                high = jnp.where(high_on, edge_in[1, at, :], 0.0)
                value = value + 0.25 * (low + high)
            return value

        def store(t, r, value):
            line_out[pl.ds(t * rows + r, 8, stride=seg * rows), :] = value

        solve_lines(load, store, seg)

        def give(i, carry):
            z = lax.rem(pz + far_first(lax.div(i, 2 * cx), cz), cz)
            x = lax.rem(px + far_first(lax.rem(lax.div(i, 2), cx), cx), cx)
            to = gx_of(x, z, lax.rem(i, 2))
            src = line_out.at[pl.ds(pl.multiple_of(to * rows, rows), rows)]
            dst = line_in.at[pl.ds(pl.multiple_of(mine * rows, rows), rows)]

            @pl.when(to == gx)
            def _():
                pltpu.make_async_copy(src, dst, recv_sem.at[5]).start()

            @pl.when(to != gx)
            def _():
                remote(src, dst, 5, (to, gy)).start()

            return carry

        lax.fori_loop(0, count_x, give, 0)

    loads[6].wait()
    eye = lax.broadcasted_iota(jnp.int32, (y_cells, y_cells), 0) == lax.broadcasted_iota(
        jnp.int32, (y_cells, y_cells), 1
    )
    names = basin_ref[...].astype(F32)
    basin_idx = lax.broadcasted_iota(jnp.int32, (y_cells, basins), 1).astype(F32)
    member = []
    for x in range(rows):
        column = jnp.sum(jnp.where(eye, names[x:x + 1], 0.0), axis=1, keepdims=True)
        member.append(jnp.where(basin_idx == column, 1.0, 0.0).astype(F32))

    wait_rows(recv_sem.at[5], line_in, owners * rows)
    solved = [
        jnp.concatenate([line_in[pl.ds((k * chunks + j) * rows, rows)] for j in range(chunks)], 1)
        for k in range(3)
    ]
    change = [solved[k] - state[k] for k in range(3)]

    halos = []
    for side, step in ((0, 1), (1, -1)):
        for c in range(3):
            facing = facing_up if side == 0 else facing_down
            halo_out[side, pl.ds(c * rows, rows)] = facing(change[c])
        copy = remote(halo_out.at[side], halo_in.at[side], 2 + side, (gx, along_y(step)))
        copy.start()
        halos.append(copy)

    reach = 1
    rounds = []
    while reach < count_y // 2:
        rounds.append(reach)
        reach *= 2

    def tell(k):
        for step in (rounds[k], -rounds[k]):
            pl.semaphore_signal(
                ready_sem.at[k], inc=1, device_id=(gx, along_y(step)), device_id_type=MESH
            )

    if rounds:
        tell(0)
    acc = forc_ref[3] - block(3, 3) * state[3]
    for k in range(3):
        acc = acc - block(3, k) * solved[k]
    step = masked(acc * inv_visc)
    for k in range(3):
        smooth_ref[k] = jnp.where(active, solved[k], sol_ref[k])
    smooth_ref[3] = sol_ref[3] + step
    around = inner_neighbours(change)
    coupled = []
    for k in range(3):
        acc = block(k, 3) * step
        for j in range(3):
            if j != k:
                acc = acc + block(k, j) * change[j]
        coupled.append(acc)
    for copy in halos:
        copy.wait_recv()
    post = []
    for k in range(3):
        low = jnp.where(gy > 0, halo_in[0, pl.ds(k * rows, rows)], 0.0)
        high = jnp.where(gy < count_y - 1, halo_in[1, pl.ds(k * rows, rows)], 0.0)
        pad = jnp.zeros((rows, lanes - LANE), F32)
        beside = jnp.concatenate([low, pad], 1) + jnp.concatenate([pad, high], 1)
        post.append(masked(0.25 * visc_ref[...] * (around[k] + beside) - coupled[k]))
    post.append((visc_ref[...] - block(3, 3)) * step)
    by_row = jnp.concatenate([post[k][x:x + 1] for x in range(rows) for k in range(4)], 0)
    sums = lax.dot_general(
        by_row, spread, (((1,), (1,)), ((), ())), precision=HIGHEST, preferred_element_type=F32
    )
    for x in range(rows):
        for k in range(4):
            column_ref[k, x:x + 1, :] = sums[4 * x + k:4 * x + k + 1]
    part = jnp.dot(sums[0:4], member[0], precision=HIGHEST, preferred_element_type=F32)
    for x in range(1, rows):
        part = part + jnp.dot(
            sums[4 * x:4 * x + 4], member[x], precision=HIGHEST, preferred_element_type=F32
        )

    pieces = basins // LANE

    def packed(pair):
        return jnp.concatenate([pair[:, j * LANE:(j + 1) * LANE] for j in range(pieces)], 0)

    lower, upper = packed(part[0:2]), packed(part[2:4])
    core_out[0] = jnp.where(core == 0, upper, lower)
    first = remote(core_out.at[0], core_in.at[0], 6, (partner, gy))
    first.start()
    if rounds:
        pl.semaphore_wait(ready_sem.at[0], 2)
        for k in range(1, len(rounds)):
            tell(k)
            if k + 1 < len(rounds):
                pl.semaphore_wait(ready_sem.at[k], 2)
    first.wait_recv()
    own = jnp.where(core == 0, lower, upper) + core_in[0]
    ring_buf[pz] = own

    def to_ring(i, carry):
        z = lax.rem(pz + far_first(i, cz), cz)
        remote(ring_buf.at[pz], ring_buf.at[pz], 7, (gx_of(px, z, core), gy)).start()
        return carry

    lax.fori_loop(0, cz - 1, to_ring, 0)
    wait_rows(recv_sem.at[7], ring_buf, cz - 1)
    own = ring_buf[0]
    for i in range(1, cz):
        own = own + ring_buf[i]
    if len(rounds) > 1:
        pl.semaphore_wait(ready_sem.at[len(rounds) - 1], 2)
    here = px * count_y + gy
    plane_buf[here] = own

    def to_plane(i, carry):
        x = lax.rem(px + far_first(lax.rem(i, cx), cx), cx)
        y = lax.rem(gy + far_first(lax.div(i, cx), count_y), count_y)
        remote(plane_buf.at[here], plane_buf.at[here], 8, (gx_of(x, pz, core), y)).start()
        return carry

    lax.fori_loop(0, cx * count_y - 1, to_plane, 0)
    wait_rows(recv_sem.at[8], plane_buf, cx * count_y - 1)
    own = plane_buf[0]
    for i in range(1, cx * count_y):
        own = own + plane_buf[i]
    core_out[1] = own
    last = remote(core_out.at[1], core_in.at[1], 9, (partner, gy))
    last.start()
    last.wait_recv()
    other = core_in[1]
    lower, upper = jnp.where(core == 0, own, other), jnp.where(core == 0, other, own)
    for j in range(pieces):
        width = min(LANE, total_ref.shape[1] - j * LANE)
        if width > 0:
            total_ref[0:2, j * LANE:j * LANE + width] = lower[2 * j:2 * j + 2, :width]
            total_ref[2:4, j * LANE:j * LANE + width] = upper[2 * j:2 * j + 2, :width]

    for copy in halos + [first, last]:
        copy.wait_send()
    for side in range(2):
        wait_rows(send_sem.at[side], edge_out, 3 * rows)

    @pl.when(owning)
    def _():
        wait_rows(send_sem.at[4], row_out, (owners - 1) * wide_rows)
        wait_rows(send_sem.at[5], line_out, (count_x - 1) * rows)

    @pl.when(jnp.logical_not(owning))
    def _():
        wait_rows(send_sem.at[4], row_out, owners * wide_rows)

    wait_rows(send_sem.at[7], ring_buf, cz - 1)
    wait_rows(send_sem.at[8], plane_buf, cx * count_y - 1)


def solution(mesh):
    count_x, count_y = mesh.shape["gx"], mesh.shape["gy"]
    cx, cz = factors(count_x)

    def local(sol, forc, visc, blocks, layers, frozen, basin_map):
        rows, lanes = visc.shape
        chunks = lanes // LANE
        owners = 3 * chunks
        basins = count_x // 2 * count_y
        padded = -(-basins // LANE) * LANE
        size = 2 * padded // LANE
        vmem = pl.BlockSpec(memory_space=pltpu.VMEM)
        anywhere = pl.BlockSpec(memory_space=pl.ANY)
        results = (
            jax.ShapeDtypeStruct(sol.shape, F32),
            jax.ShapeDtypeStruct((4,) + layers.shape, F32),
            jax.ShapeDtypeStruct((4, basins), F32),
        )
        inputs = (sol, forc, visc, blocks, layers, frozen, basin_map)
        return pl.pallas_call(
            functools.partial(sweep_kernel, count_x, count_y, padded),
            out_shape=results,
            in_specs=[anywhere] * 7,
            out_specs=(vmem, vmem, vmem),
            scratch_shapes=[pltpu.VMEM(a.shape, a.dtype) for a in inputs] + [
                pltpu.VMEM((6 * rows, LANE), F32),
                pltpu.VMEM((2, count_x * rows, LANE), F32),
                pltpu.VMEM((2, 3 * rows, LANE), F32),
                pltpu.VMEM((2, 3 * rows, LANE), F32),
                pltpu.VMEM((owners * 2 * rows, LANE), F32),
                pltpu.VMEM((count_x * 2 * rows, LANE), F32),
                pltpu.VMEM((count_x * rows, LANE), F32),
                pltpu.VMEM((owners * rows, LANE), F32),
                pltpu.VMEM((2, size, LANE), F32),
                pltpu.VMEM((2, size, LANE), F32),
                pltpu.VMEM((cz, size, LANE), F32),
                pltpu.VMEM((cx * count_y, size, LANE), F32),
                pltpu.SemaphoreType.DMA((7,)),
                pltpu.SemaphoreType.DMA((10,)),
                pltpu.SemaphoreType.DMA((10,)),
                pltpu.SemaphoreType.REGULAR((4,)),
            ],
            compiler_params=pltpu.CompilerParams(
                collective_id=0, has_side_effects=True, vmem_limit_bytes=63 * 2**20
            ),
            name="sweep",
        )(*inputs)
    return jax.shard_map(
        local,
        mesh=mesh,
        in_specs=(
            P(None, "gx", "gy"), P(None, "gx", "gy"), P("gx", "gy"), P(None, "gx", "gy"),
            P("gx", "gy"), P("gx", "gy"), P("gx", "gy"),
        ),
        out_specs=(P(None, "gx", "gy"), P(None, "gx", "gy"), P()),
        check_vma=False,
    )
```

```python
import functools

import jax
import jax.numpy as jnp
from jax import lax
from jax.experimental import pallas as pl
from jax.experimental.pallas import tpu as pltpu
from jax.sharding import PartitionSpec as P

MESH = pl.DeviceIdType.MESH
HIGHEST = lax.Precision.HIGHEST
F32 = jnp.float32
LANE = 128
SKIP = 3


def factors(count_x):
    return (4, count_x // 8) if count_x == 96 else (2, count_x // 4)


def roll(value, shift, axis=1):
    size = value.shape[axis]
    return pltpu.roll(value, shift % size, axis)


def eliminate_levels(count):
    left = list(range(count))
    levels = []
    while len(left) > 1:
        gone = [pos for pos in range(0, len(left) - 1, 2)]
        levels.append([(left[p], left[p - 1] if p else None, left[p + 1]) for p in gone])
        left = [cell for pos, cell in enumerate(left) if pos not in gone]
    return levels


def reduce_lines(load, count):
    sub = lax.broadcasted_iota(jnp.int32, (8, LANE), 0)
    first, last = sub == 0, sub == 7
    one, zero = jnp.full((8, LANE), 1.0, F32), jnp.zeros((8, LANE), F32)
    d0, d1, r0, r1 = ([load(t, q) for t in range(count)] for q in range(4))
    on0 = [d >= 0.0 for d in d0]
    on1 = [d >= 0.0 for d in d1]
    r0 = [jnp.where(on, r, zero) for on, r in zip(on0, r0)]
    r1 = [jnp.where(on, r, zero) for on, r in zip(on1, r1)]
    flag1 = [jnp.where(on, one, zero) for on in on1]
    before = [jnp.where(first, one, roll(flag1[-1], 1, 0))] + flag1[:-1]
    edge_in = [jnp.where(on, b, zero) for on, b in zip(on0, before)]
    edge_mid = [jnp.where(on, f, zero) for on, f in zip(on0, flag1)]
    edge_out = edge_in[1:] + [jnp.where(last, one, roll(edge_in[0], -1, 0))]
    leak0 = [jnp.where(on, d + (2.0 - a - b), one) for on, d, a, b in zip(on0, d0, edge_in, edge_mid)]
    leak1 = [jnp.where(on, d + (2.0 - a - b), one) for on, d, a, b in zip(on1, d1, edge_mid, edge_out)]
    out_leak = jnp.where(last, roll(jnp.where(on0[0], zero, one), -1, 0), zero)
    out_src = zero
    inv0 = [1.0 / (d + (a + b)) for d, a, b in zip(leak0, edge_in, edge_mid)]
    part_leak = [d * i for d, i in zip(leak0, inv0)]
    part_src = [r * i for r, i in zip(r0, inv0)]
    give_leak = [e * p for e, p in zip(edge_in, part_leak)]
    give_src = [e * p for e, p in zip(edge_in, part_src)]
    low_leak, low_src = roll(give_leak[0], -1, 0), roll(give_src[0], -1, 0)
    out_leak, out_src = out_leak + low_leak, out_src + low_src
    give_leak = give_leak[1:] + [jnp.where(last, zero, low_leak)]
    give_src = give_src[1:] + [jnp.where(last, zero, low_src)]
    leak = [d + (e * p + g) for d, e, p, g in zip(leak1, edge_mid, part_leak, give_leak)]
    src = [r + (e * p + g) for r, e, p, g in zip(r1, edge_mid, part_src, give_src)]
    edge = [a * (b * i) for a, b, i in zip(edge_in, edge_mid, inv0)]
    kept = {}
    for level in eliminate_levels(count):
        updates = []
        for cell, low, high in level:
            lo_edge, hi_edge = edge[cell], edge[high]
            inv = 1.0 / (leak[cell] + (lo_edge + hi_edge))
            lo_share, hi_share = lo_edge * inv, hi_edge * inv
            kept[cell] = (lo_share, hi_share, src[cell] * inv)
            updates.append((cell, low, high, lo_edge * hi_share, lo_share, hi_share))
        for cell, low, high, joined, lo_share, hi_share in updates:
            low_leak, low_src = lo_share * leak[cell], lo_share * src[cell]
            if low is None:
                low_leak, low_src = roll(low_leak, -1, 0), roll(low_src, -1, 0)
                out_leak, out_src = out_leak + low_leak, out_src + low_src
                low, low_leak, low_src = count - 1, jnp.where(last, zero, low_leak), jnp.where(last, zero, low_src)
            leak[low], src[low] = leak[low] + low_leak, src[low] + low_src
            leak[high], src[high] = leak[high] + hi_share * leak[cell], src[high] + hi_share * src[cell]
            edge[high] = joined
    end_leak, end_src, lo_edge = leak[-1], src[-1], edge[-1]
    hi_edge = jnp.where(last, zero, roll(lo_edge, -1, 0))
    hops = []
    for hop in (1, 2, 4):
        gone = lax.rem(sub, 2 * hop) == hop - 1
        inv = 1.0 / jnp.where(gone, end_leak + (lo_edge + hi_edge), one)
        lo_share = jnp.where(gone, lo_edge * inv, zero)
        hi_share = jnp.where(gone, hi_edge * inv, zero)
        hops.append((hop, gone, lo_share, hi_share, end_src * inv))
        low_leak, low_src = roll(lo_share * end_leak, -hop, 0), roll(lo_share * end_src, -hop, 0)
        out_leak, out_src = out_leak + low_leak, out_src + low_src
        joined = lo_edge * hi_share
        end_leak, end_src = (
            end_leak + (jnp.where(last, zero, low_leak) + roll(hi_share * end_leak, hop, 0)),
            end_src + (jnp.where(last, zero, low_src) + roll(hi_share * end_src, hop, 0)),
        )
        lo_edge, hi_edge = roll(joined, hop, 0), jnp.where(last, zero, roll(joined, -hop, 0))
    end_leak = jnp.where(on1[-1], end_leak, -one)

    def back(own, previous):
        ends = jnp.where(last, own, zero)
        for hop, gone, lo_share, hi_share, value in reversed(hops):
            lower = jnp.where(sub < hop, previous, roll(ends, hop, 0))
            ends = jnp.where(gone, value + (lo_share * lower + hi_share * roll(ends, -hop, 0)), ends)
        value = [None] * count
        value[-1] = ends
        wrapped = jnp.where(first, previous, roll(ends, 1, 0))
        for level in reversed(eliminate_levels(count)):
            for cell, low, high in level:
                lo_share, hi_share, part = kept[cell]
                lower = wrapped if low is None else value[low]
                value[cell] = part + (lo_share * lower + hi_share * value[high])
        pairs = []
        for t in range(count):
            lower = wrapped if t == 0 else value[t - 1]
            pairs.append((part_src[t] + (edge_in[t] * lower + edge_mid[t] * value[t]) * inv0[t], value[t]))
        return pairs

    return (end_leak, end_src, lo_edge, out_leak, out_src), back


def solve_ends(groups):
    count = len(groups)
    on = [g[0] >= 0.0 for g in groups]
    edges = [jnp.zeros_like(groups[0][0])]
    for i in range(1, count):
        edges.append(jnp.where(jnp.logical_and(on[i - 1], on[i]), groups[i][2], 0.0))
    leaks, srcs = [], []
    for i in range(count):
        leak, src, lo_edge = groups[i][:3]
        leak = leak + (lo_edge - edges[i])
        if i + 1 < count:
            leak = leak + (groups[i + 1][3] + (groups[i + 1][2] - edges[i + 1]))
            src = src + groups[i + 1][4]
        else:
            leak = leak + 1.0
        leaks.append(jnp.where(on[i], leak, 1.0))
        srcs.append(jnp.where(on[i], src, 0.0))
    inverse = []
    for i in range(count):
        if i + 1 < count:
            inv = 1.0 / (leaks[i] + edges[i + 1])
            share = edges[i + 1] * inv
            leaks[i + 1] = leaks[i + 1] + share * leaks[i]
            srcs[i + 1] = srcs[i + 1] + share * srcs[i]
        else:
            inv = 1.0 / leaks[i]
        inverse.append(inv)
    values = [None] * count
    values[-1] = srcs[-1] * inverse[-1]
    for i in reversed(range(count - 1)):
        values[i] = (srcs[i] + edges[i + 1] * values[i + 1]) * inverse[i]
    return values


def far_first(i, count):
    side = 1 - 2 * lax.rem(i, 2)
    return count // 2 + side * lax.div(i + 1, 2)


def sweep_kernel(
    count_x, count_y, basins,
    sol_hbm, forc_hbm, visc_hbm, blk_hbm, layers_hbm, frozen_hbm, basin_hbm,
    smooth_ref, column_ref, total_ref,
    sol_ref, forc_ref, visc_ref, blk_ref, layers_ref, frozen_ref, basin_ref,
    edge_out, edge_in, side_out, side_in, halo_out, halo_in, row_out, row_in, line_out, line_in, ends_buf,
    core_out, core_in, ring_buf, plane_buf, load_sem, send_sem, recv_sem, ready_sem,
):
    cx, cz = factors(count_x)
    rows, lanes = visc_ref.shape
    y_cells = layers_ref.shape[1]
    layers = lanes // y_cells
    chunks = lanes // LANE
    group = 2 * cz
    seg = group // 8
    gx, gy = lax.axis_index("gx"), lax.axis_index("gy")
    core = lax.rem(gx, 2)
    pz = lax.rem(lax.div(gx, 2), cz)
    px = lax.div(gx, 2 * cz)
    partner = gx + 1 - 2 * core
    skip = min(SKIP, group - chunks)
    place = 2 * pz + core - skip
    owning = jnp.logical_and(place >= 0, place < chunks)
    low_edge = jnp.logical_and(owning, place == 0)
    high_edge = jnp.logical_and(owning, place == 1)
    order = [0, chunks - 1] + list(range(1, chunks - 1))
    place_of = {chunk: i for i, chunk in enumerate(order)}
    member = 2 * pz + core

    def along_y(step):
        return lax.rem(gy + step + count_y, count_y)

    def gx_of(x, z, c):
        return (x * cz + z) * 2 + c

    def owner_of(place):
        return gx_of(px, lax.div(place + skip, 2), lax.rem(place + skip, 2))

    loads = [
        pltpu.make_async_copy(src, dst, load_sem.at[i])
        for i, (src, dst) in enumerate((
            (layers_hbm, layers_ref), (frozen_hbm, frozen_ref), (sol_hbm, sol_ref),
            (visc_hbm, visc_ref), (blk_hbm, blk_ref), (forc_hbm, forc_ref), (basin_hbm, basin_ref),
        ))
    ]
    for copy in loads:
        copy.start()

    barrier = pltpu.get_barrier_semaphore()

    def greet(y):
        def one(i, carry):
            to = gx_of(px, cz - 1 - lax.div(i, 2), lax.rem(i, 2))

            @pl.when(jnp.logical_or(to != gx, y != gy))
            def _():
                pl.semaphore_signal(barrier, inc=1, device_id=(to, y), device_id_type=MESH)

            return carry

        return one

    @pl.when(owning)
    def _():
        lax.fori_loop(0, group, greet(gy), 0)
        for i in range(1, cx):
            pl.semaphore_signal(
                barrier, inc=1, device_id=(gx_of(lax.rem(px + i, cx), pz, core), gy),
                device_id_type=MESH,
            )

    @pl.when(low_edge)
    def _():
        lax.fori_loop(0, group, greet(along_y(-1)), 0)

    @pl.when(high_edge)
    def _():
        lax.fori_loop(0, group, greet(along_y(1)), 0)

    def remote(src, dst, k, to):
        return pltpu.make_async_remote_copy(
            src_ref=src, dst_ref=dst, send_sem=send_sem.at[k], recv_sem=recv_sem.at[k],
            device_id=to, device_id_type=MESH,
        )

    def wait_rows(sem, ref, count):
        view = ref.at[pl.ds(0, count)]
        pltpu.make_async_copy(view, view, sem).wait()

    for step in (1, -1):
        pl.semaphore_signal(barrier, inc=1, device_id=(gx, along_y(step)), device_id_type=MESH)

    lane = lax.broadcasted_iota(jnp.int32, (rows, lanes), 1)

    def cell_of(index):
        return ((index.astype(F32) + 0.5) * (1.0 / layers)).astype(jnp.int32)

    layer = lane - cell_of(lane) * layers
    wide = lax.broadcasted_iota(jnp.int32, (y_cells, lanes), 1)
    spread = jnp.where(
        cell_of(wide) == lax.broadcasted_iota(jnp.int32, (y_cells, lanes), 0), 1.0, 0.0
    ).astype(F32)
    loads[0].wait()
    loads[1].wait()
    filled = jnp.dot(layers_ref[...].astype(F32), spread, precision=HIGHEST, preferred_element_type=F32)
    frozen = jnp.dot(frozen_ref[...].astype(F32), spread, precision=HIGHEST, preferred_element_type=F32)
    active = layer.astype(F32) + 0.5 < filled
    bottom, top = layer == 0, layer == layers - 1
    slide = 1.0 - frozen

    def masked(value):
        return jnp.where(active, value, 0.0)

    loads[2].wait()
    state = [masked(sol_ref[k]) for k in range(4)]
    small = lax.broadcasted_iota(jnp.int32, (rows, LANE), 1)

    def facing_up(value):
        return jnp.where(small < layers, roll(value[:, lanes - LANE:], layers), 0.0)

    def facing_down(value):
        return jnp.where(small >= LANE - layers, roll(value[:, :LANE], LANE - layers), 0.0)

    def inner_neighbours(values):
        out = []
        for v in values:
            before = jnp.where(lane < layers, 0.0, roll(v, layers))
            after = jnp.where(lane >= lanes - layers, 0.0, roll(v, lanes - layers))
            below = jnp.where(bottom, v * slide, roll(v, 1))
            above = jnp.where(top, 0.0, roll(v, lanes - 1))
            out.append((before + after) + (below + above))
        return out

    def block(k, j):
        return blk_ref[4 * k + j]

    for k in range(3):
        edge_out[0, pl.ds(k * rows, rows)] = facing_up(state[k])
        edge_out[1, pl.ds(k * rows, rows)] = facing_down(state[k])
    around = inner_neighbours(state[:3])
    wide_rows = 2 * rows
    loads[6].wait()
    names = basin_ref[...].astype(F32)
    for side, column in ((0, y_cells - 1), (1, 0)):
        side_out[side, pl.ds(rows, rows)] = jnp.broadcast_to(names[:, column:column + 1], (rows, LANE))
    loads[3].wait()
    weight = masked(0.25 * visc_ref[...])
    side_out[0, pl.ds(0, rows)] = facing_up(weight)
    side_out[1, pl.ds(0, rows)] = facing_down(weight)
    loads[4].wait()
    loads[5].wait()
    inv_visc = 1.0 / visc_ref[...]
    for k in range(3):
        acc = forc_ref[k]
        for j in range(4):
            if j != k:
                acc = acc - block(k, j) * state[j]
        rhs = masked(acc * inv_visc + 0.25 * around[k])
        diag = jnp.where(active, block(k, k) * inv_visc, -1.0)
        for j in range(chunks):
            at = place_of[j] * 16 + k * wide_rows
            row_out[pl.ds(at, rows)] = diag[:, j * LANE:(j + 1) * LANE]
            row_out[pl.ds(at + rows, rows)] = rhs[:, j * LANE:(j + 1) * LANE]

    @pl.when(owning)
    def _():
        pl.semaphore_wait(barrier, chunks - 1 + 4 + cx - 1)

    @pl.when(jnp.logical_not(owning))
    def _():
        pl.semaphore_wait(barrier, chunks + 4)

    def to_owner(i, carry):
        at = chunks - 1 - i
        to = owner_of(at)
        src = row_out.at[pl.ds(pl.multiple_of(at * 16, 16), 3 * wide_rows)]
        dst = row_in.at[pl.ds(pl.multiple_of(member * 16, 16), 3 * wide_rows)]

        @pl.when(to == gx)
        def _():
            pltpu.make_async_copy(src, dst, recv_sem.at[4]).start()

        @pl.when(to != gx)
        def _():
            remote(src, dst, 4, (to, gy)).start()

        return carry

    for side, step in ((0, 1), (1, -1)):
        remote(
            edge_out.at[side],
            edge_in.at[side, pl.ds(pl.multiple_of(member * 8, 8), 8)],
            side, (owner_of(side), along_y(step)),
        ).start()
    lax.fori_loop(0, chunks, to_owner, 0)

    sides = []
    for side, step in ((0, 1), (1, -1)):
        copy = remote(side_out.at[side], side_in.at[side], 11 + side, (gx, along_y(step)))
        copy.start()
        sides.append(copy)

    @pl.when(owning)
    def _():
        @pl.when(low_edge)
        def _():
            wait_rows(recv_sem.at[0], edge_in.at[0], group * 8)

        @pl.when(high_edge)
        def _():
            wait_rows(recv_sem.at[1], edge_in.at[1], group * 8)

        wait_rows(recv_sem.at[4], row_in, group * 3 * wide_rows)
        low_on = jnp.logical_and(low_edge, gy > 0)
        high_on = jnp.logical_and(high_edge, gy < count_y - 1)
        ways = []
        for k in range(3):
            def load(t, q, k=k):
                value = row_in[pl.ds(t * 16 + k * wide_rows + q, 8, stride=seg * 16), :]
                if q >= rows:
                    at = pl.ds(t * 8 + k * rows + q - rows, 8, stride=seg * 8)
                    low = jnp.where(low_on, edge_in[0, at, :], 0.0)
                    high = jnp.where(high_on, edge_in[1, at, :], 0.0)
                    value = value + 0.25 * (low + high)
                return value

            found, back = reduce_lines(load, seg)
            for i, value in enumerate(found):
                ends_buf[px, 3 * i + k:3 * i + k + 1] = value[7:8]
            ways.append(back)

        for i in range(cx - 1):
            x = lax.rem(px + far_first(i, cx), cx)
            remote(ends_buf.at[px], ends_buf.at[px], 10, (gx_of(x, pz, core), gy)).start()
        wait_rows(recv_sem.at[10], ends_buf, cx - 1)
        ends = solve_ends([[ends_buf[x, 3 * i:3 * i + 3] for i in range(5)] for x in range(cx)])
        own, previous = jnp.zeros((3, LANE), F32), jnp.zeros((3, LANE), F32)
        for x in range(cx):
            own = jnp.where(px == x, ends[x], own)
            previous = jnp.where(px == x + 1, ends[x], previous)
        for k in range(3):
            for t, pair in enumerate(ways[k](own[k:k + 1], previous[k:k + 1])):
                for r in range(rows):
                    line_out[pl.ds(t * 8 + k * rows + r, 8, stride=seg * 8), :] = pair[r]

        def give(i, carry):
            z = lax.rem(pz + far_first(lax.div(i, 2), cz), cz)
            m = 2 * z + lax.rem(i, 2)
            to = gx_of(px, z, lax.rem(i, 2))
            src = line_out.at[pl.ds(pl.multiple_of(m * 8, 8), 3 * rows)]
            dst = line_in.at[pl.ds(pl.multiple_of(place * 8, 8), 3 * rows)]

            @pl.when(to == gx)
            def _():
                pltpu.make_async_copy(src, dst, recv_sem.at[5]).start()

            @pl.when(to != gx)
            def _():
                remote(src, dst, 5, (to, gy)).start()

            return carry

        lax.fori_loop(0, group, give, 0)

    eye = lax.broadcasted_iota(jnp.int32, (y_cells, y_cells), 0) == lax.broadcasted_iota(
        jnp.int32, (y_cells, y_cells), 1
    )
    basin_idx = lax.broadcasted_iota(jnp.int32, (y_cells, basins), 1).astype(F32)
    belongs = []
    for x in range(rows):
        column = jnp.sum(jnp.where(eye, names[x:x + 1], 0.0), axis=1, keepdims=True)
        belongs.append(jnp.where(basin_idx == column, 1.0, 0.0).astype(F32))

    for copy in sides:
        copy.wait_recv()
    wait_rows(recv_sem.at[5], line_in, chunks * 3 * rows)
    solved = [
        jnp.concatenate([line_in[pl.ds(place_of[j] * 8 + k * rows, rows)] for j in range(chunks)], 1)
        for k in range(3)
    ]
    change = [solved[k] - state[k] for k in range(3)]

    beside = []
    for side, on in ((0, gy > 0), (1, gy < count_y - 1)):
        given = jnp.where(on, side_in[side, pl.ds(0, rows)], 0.0)
        at = (lanes - LANE) * side
        beside.append([
            jnp.sum(given * change[k][:, at:at + LANE], axis=1, keepdims=True) for k in range(3)
        ])
    halos = []
    for side, step in ((0, 1), (1, -1)):
        for k in range(3):
            halo_out[side, pl.ds(k * rows, rows)] = jnp.broadcast_to(beside[1 - side][k], (rows, LANE))
        copy = remote(halo_out.at[side], halo_in.at[side], 2 + side, (gx, along_y(step)))
        copy.start()
        halos.append(copy)

    reach = 1
    rounds = []
    while reach < count_y // 2:
        rounds.append(reach)
        reach *= 2

    def tell(k):
        for step in (rounds[k], -rounds[k]):
            pl.semaphore_signal(
                ready_sem.at[k], inc=1, device_id=(gx, along_y(step)), device_id_type=MESH
            )

    if rounds:
        tell(0)
    acc = forc_ref[3] - block(3, 3) * state[3]
    for k in range(3):
        acc = acc - block(3, k) * solved[k]
    step = masked(acc * inv_visc)
    for k in range(3):
        smooth_ref[k] = jnp.where(active, solved[k], sol_ref[k])
    smooth_ref[3] = sol_ref[3] + step
    around = inner_neighbours(change)
    coupled = []
    for k in range(3):
        acc = block(k, 3) * step
        for j in range(3):
            if j != k:
                acc = acc + block(k, j) * change[j]
        coupled.append(acc)
    post = [masked(0.25 * visc_ref[...] * around[k] - coupled[k]) for k in range(3)]
    post.append((visc_ref[...] - block(3, 3)) * step)
    by_row = jnp.concatenate([post[k][x:x + 1] for x in range(rows) for k in range(4)], 0)
    sums = lax.dot_general(
        by_row, spread, (((1,), (1,)), ((), ())), precision=HIGHEST, preferred_element_type=F32
    )
    part = jnp.dot(sums[0:4], belongs[0], precision=HIGHEST, preferred_element_type=F32)
    for x in range(1, rows):
        part = part + jnp.dot(
            sums[4 * x:4 * x + 4], belongs[x], precision=HIGHEST, preferred_element_type=F32
        )

    index4 = lax.broadcasted_iota(jnp.int32, (4, basins), 1).astype(F32)
    for side in range(2):
        for x in range(rows):
            amount = jnp.concatenate(
                [beside[side][k][x:x + 1] for k in range(3)] + [jnp.zeros((1, 1), F32)], 0
            )
            name = side_in[side, rows + x:rows + x + 1, 0:1]
            part = part + jnp.where(index4 == name, amount, 0.0)

    pieces = basins // LANE

    def packed(pair):
        return jnp.concatenate([pair[:, j * LANE:(j + 1) * LANE] for j in range(pieces)], 0)

    lower, upper = packed(part[0:2]), packed(part[2:4])
    core_out[0] = jnp.where(core == 0, upper, lower)
    first = remote(core_out.at[0], core_in.at[0], 6, (partner, gy))
    first.start()
    if rounds:
        pl.semaphore_wait(ready_sem.at[0], 2)
        for k in range(1, len(rounds)):
            tell(k)
            if k + 1 < len(rounds):
                pl.semaphore_wait(ready_sem.at[k], 2)
    first.wait_recv()
    own = jnp.where(core == 0, lower, upper) + core_in[0]
    ring_buf[pz] = own

    def to_ring(i, carry):
        z = lax.rem(pz + far_first(i, cz), cz)
        remote(ring_buf.at[pz], ring_buf.at[pz], 7, (gx_of(px, z, core), gy)).start()
        return carry

    lax.fori_loop(0, cz - 1, to_ring, 0)
    for copy in halos:
        copy.wait_recv()
    column_idx = lax.broadcasted_iota(jnp.int32, (1, y_cells), 1)
    for x in range(rows):
        for k in range(4):
            value = sums[4 * x + k:4 * x + k + 1]
            if k < 3:
                at = k * rows + x
                low, high = (halo_in[side, at:at + 1, 0:y_cells] for side in range(2))
                value = value + jnp.where(column_idx == 0, low, 0.0)
                value = value + jnp.where(column_idx == y_cells - 1, high, 0.0)
            column_ref[k, x:x + 1, :] = value
    wait_rows(recv_sem.at[7], ring_buf, cz - 1)
    own = ring_buf[0]
    for i in range(1, cz):
        own = own + ring_buf[i]
    if len(rounds) > 1:
        pl.semaphore_wait(ready_sem.at[len(rounds) - 1], 2)
    here = px * count_y + gy
    plane_buf[here] = own

    def to_plane(i, carry):
        x = lax.rem(px + far_first(lax.rem(i, cx), cx), cx)
        y = lax.rem(gy + far_first(lax.div(i, cx), count_y), count_y)
        remote(plane_buf.at[here], plane_buf.at[here], 8, (gx_of(x, pz, core), y)).start()
        return carry

    lax.fori_loop(0, cx * count_y - 1, to_plane, 0)
    wait_rows(recv_sem.at[8], plane_buf, cx * count_y - 1)
    own = plane_buf[0]
    for i in range(1, cx * count_y):
        own = own + plane_buf[i]
    core_out[1] = own
    last = remote(core_out.at[1], core_in.at[1], 9, (partner, gy))
    last.start()
    last.wait_recv()
    other = core_in[1]
    lower, upper = jnp.where(core == 0, own, other), jnp.where(core == 0, other, own)
    for j in range(pieces):
        width = min(LANE, total_ref.shape[1] - j * LANE)
        if width > 0:
            total_ref[0:2, j * LANE:j * LANE + width] = lower[2 * j:2 * j + 2, :width]
            total_ref[2:4, j * LANE:j * LANE + width] = upper[2 * j:2 * j + 2, :width]

    for copy in sides + halos + [first, last]:
        copy.wait_send()
    for side in range(2):
        wait_rows(send_sem.at[side], edge_out.at[side], 8)

    @pl.when(owning)
    def _():
        wait_rows(send_sem.at[4], row_out, (chunks - 1) * 3 * wide_rows)
        wait_rows(send_sem.at[5], line_out, (group - 1) * 3 * rows)
        wait_rows(send_sem.at[10], ends_buf, cx - 1)

    @pl.when(jnp.logical_not(owning))
    def _():
        wait_rows(send_sem.at[4], row_out, chunks * 3 * wide_rows)

    wait_rows(send_sem.at[7], ring_buf, cz - 1)
    wait_rows(send_sem.at[8], plane_buf, cx * count_y - 1)


def solution(mesh):
    count_x, count_y = mesh.shape["gx"], mesh.shape["gy"]
    cx, cz = factors(count_x)

    def local(sol, forc, visc, blocks, layers, frozen, basin_map):
        rows, lanes = visc.shape
        chunks = lanes // LANE
        basins = count_x // 2 * count_y
        padded = -(-basins // LANE) * LANE
        size = 2 * padded // LANE
        vmem = pl.BlockSpec(memory_space=pltpu.VMEM)
        anywhere = pl.BlockSpec(memory_space=pl.ANY)
        results = (
            jax.ShapeDtypeStruct(sol.shape, F32),
            jax.ShapeDtypeStruct((4,) + layers.shape, F32),
            jax.ShapeDtypeStruct((4, basins), F32),
        )
        inputs = (sol, forc, visc, blocks, layers, frozen, basin_map)
        return pl.pallas_call(
            functools.partial(sweep_kernel, count_x, count_y, padded),
            out_shape=results,
            in_specs=[anywhere] * 7,
            out_specs=(vmem, vmem, vmem),
            scratch_shapes=[pltpu.VMEM(a.shape, a.dtype) for a in inputs] + [
                pltpu.VMEM((2, 8, LANE), F32),
                pltpu.VMEM((2, 2 * cz * 8, LANE), F32),
                pltpu.VMEM((2, 2 * rows, LANE), F32),
                pltpu.VMEM((2, 2 * rows, LANE), F32),
                pltpu.VMEM((2, 3 * rows, LANE), F32),
                pltpu.VMEM((2, 3 * rows, LANE), F32),
                pltpu.VMEM((chunks * 16, LANE), F32),
                pltpu.VMEM((2 * cz * 16, LANE), F32),
                pltpu.VMEM((2 * cz * 8, LANE), F32),
                pltpu.VMEM((chunks * 8, LANE), F32),
                pltpu.VMEM((cx, 16, LANE), F32),
                pltpu.VMEM((2, size, LANE), F32),
                pltpu.VMEM((2, size, LANE), F32),
                pltpu.VMEM((cz, size, LANE), F32),
                pltpu.VMEM((cx * count_y, size, LANE), F32),
                pltpu.SemaphoreType.DMA((7,)),
                pltpu.SemaphoreType.DMA((13,)),
                pltpu.SemaphoreType.DMA((13,)),
                pltpu.SemaphoreType.REGULAR((4,)),
            ],
            compiler_params=pltpu.CompilerParams(
                collective_id=0, has_side_effects=True, vmem_limit_bytes=63 * 2**20
            ),
            name="sweep",
        )(*inputs)
    return jax.shard_map(
        local,
        mesh=mesh,
        in_specs=(
            P(None, "gx", "gy"), P(None, "gx", "gy"), P("gx", "gy"), P(None, "gx", "gy"),
            P("gx", "gy"), P("gx", "gy"), P("gx", "gy"),
        ),
        out_specs=(P(None, "gx", "gy"), P(None, "gx", "gy"), P()),
        check_vma=False,
    )
```

```python
import functools

import jax
import jax.numpy as jnp
from jax import lax
from jax.experimental import pallas as pl
from jax.experimental.pallas import tpu as pltpu
from jax.sharding import PartitionSpec as P

MESH = pl.DeviceIdType.MESH
HIGHEST = lax.Precision.HIGHEST
F32 = jnp.float32
LANE = 128
SEATS = (1, 2, 3, 5, 6, 8, 10, 11, 13, 15)


def factors(count_x):
    return (4, count_x // 8) if count_x == 96 else (2, count_x // 4)


def roll(value, shift, axis=1):
    size = value.shape[axis]
    return pltpu.roll(value, shift % size, axis)


def eliminate_levels(count):
    left = list(range(count))
    levels = []
    while len(left) > 1:
        gone = [pos for pos in range(0, len(left) - 1, 2)]
        levels.append([(left[p], left[p - 1] if p else None, left[p + 1]) for p in gone])
        left = [cell for pos, cell in enumerate(left) if pos not in gone]
    return levels


def reduce_lines(load, count):
    sub = lax.broadcasted_iota(jnp.int32, (8, LANE), 0)
    first, last = sub == 0, sub == 7
    one, zero = jnp.full((8, LANE), 1.0, F32), jnp.zeros((8, LANE), F32)
    d0, d1, r0, r1 = ([load(t, q) for t in range(count)] for q in range(4))
    on0 = [d >= 0.0 for d in d0]
    on1 = [d >= 0.0 for d in d1]
    r0 = [jnp.where(on, r, zero) for on, r in zip(on0, r0)]
    r1 = [jnp.where(on, r, zero) for on, r in zip(on1, r1)]
    flag1 = [jnp.where(on, one, zero) for on in on1]
    before = [jnp.where(first, one, roll(flag1[-1], 1, 0))] + flag1[:-1]
    edge_in = [jnp.where(on, b, zero) for on, b in zip(on0, before)]
    edge_mid = [jnp.where(on, f, zero) for on, f in zip(on0, flag1)]
    edge_out = edge_in[1:] + [jnp.where(last, one, roll(edge_in[0], -1, 0))]
    leak0 = [jnp.where(on, d + (2.0 - a - b), one) for on, d, a, b in zip(on0, d0, edge_in, edge_mid)]
    leak1 = [jnp.where(on, d + (2.0 - a - b), one) for on, d, a, b in zip(on1, d1, edge_mid, edge_out)]
    out_leak = jnp.where(last, roll(jnp.where(on0[0], zero, one), -1, 0), zero)
    out_src = zero
    inv0 = [1.0 / (d + (a + b)) for d, a, b in zip(leak0, edge_in, edge_mid)]
    part_leak = [d * i for d, i in zip(leak0, inv0)]
    part_src = [r * i for r, i in zip(r0, inv0)]
    give_leak = [e * p for e, p in zip(edge_in, part_leak)]
    give_src = [e * p for e, p in zip(edge_in, part_src)]
    low_leak, low_src = roll(give_leak[0], -1, 0), roll(give_src[0], -1, 0)
    out_leak, out_src = out_leak + low_leak, out_src + low_src
    give_leak = give_leak[1:] + [jnp.where(last, zero, low_leak)]
    give_src = give_src[1:] + [jnp.where(last, zero, low_src)]
    leak = [d + (e * p + g) for d, e, p, g in zip(leak1, edge_mid, part_leak, give_leak)]
    src = [r + (e * p + g) for r, e, p, g in zip(r1, edge_mid, part_src, give_src)]
    edge = [a * (b * i) for a, b, i in zip(edge_in, edge_mid, inv0)]
    kept = {}
    for level in eliminate_levels(count):
        updates = []
        for cell, low, high in level:
            lo_edge, hi_edge = edge[cell], edge[high]
            inv = 1.0 / (leak[cell] + (lo_edge + hi_edge))
            lo_share, hi_share = lo_edge * inv, hi_edge * inv
            kept[cell] = (lo_share, hi_share, src[cell] * inv)
            updates.append((cell, low, high, lo_edge * hi_share, lo_share, hi_share))
        for cell, low, high, joined, lo_share, hi_share in updates:
            low_leak, low_src = lo_share * leak[cell], lo_share * src[cell]
            if low is None:
                low_leak, low_src = roll(low_leak, -1, 0), roll(low_src, -1, 0)
                out_leak, out_src = out_leak + low_leak, out_src + low_src
                low, low_leak, low_src = count - 1, jnp.where(last, zero, low_leak), jnp.where(last, zero, low_src)
            leak[low], src[low] = leak[low] + low_leak, src[low] + low_src
            leak[high], src[high] = leak[high] + hi_share * leak[cell], src[high] + hi_share * src[cell]
            edge[high] = joined
    end_leak, end_src, lo_edge = leak[-1], src[-1], edge[-1]
    hi_edge = jnp.where(last, zero, roll(lo_edge, -1, 0))
    hops = []
    for hop in (1, 2, 4):
        gone = lax.rem(sub, 2 * hop) == hop - 1
        inv = 1.0 / jnp.where(gone, end_leak + (lo_edge + hi_edge), one)
        lo_share = jnp.where(gone, lo_edge * inv, zero)
        hi_share = jnp.where(gone, hi_edge * inv, zero)
        hops.append((hop, gone, lo_share, hi_share, end_src * inv))
        low_leak, low_src = roll(lo_share * end_leak, -hop, 0), roll(lo_share * end_src, -hop, 0)
        out_leak, out_src = out_leak + low_leak, out_src + low_src
        joined = lo_edge * hi_share
        end_leak, end_src = (
            end_leak + (jnp.where(last, zero, low_leak) + roll(hi_share * end_leak, hop, 0)),
            end_src + (jnp.where(last, zero, low_src) + roll(hi_share * end_src, hop, 0)),
        )
        lo_edge, hi_edge = roll(joined, hop, 0), jnp.where(last, zero, roll(joined, -hop, 0))
    end_leak = jnp.where(on1[-1], end_leak, -one)

    def back(own, previous):
        ends = jnp.where(last, own, zero)
        for hop, gone, lo_share, hi_share, value in reversed(hops):
            lower = jnp.where(sub < hop, previous, roll(ends, hop, 0))
            ends = jnp.where(gone, value + (lo_share * lower + hi_share * roll(ends, -hop, 0)), ends)
        value = [None] * count
        value[-1] = ends
        wrapped = jnp.where(first, previous, roll(ends, 1, 0))
        for level in reversed(eliminate_levels(count)):
            for cell, low, high in level:
                lo_share, hi_share, part = kept[cell]
                lower = wrapped if low is None else value[low]
                value[cell] = part + (lo_share * lower + hi_share * value[high])
        pairs = []
        for t in range(count):
            lower = wrapped if t == 0 else value[t - 1]
            pairs.append((part_src[t] + (edge_in[t] * lower + edge_mid[t] * value[t]) * inv0[t], value[t]))
        return pairs

    return (end_leak, end_src, lo_edge, out_leak, out_src), back


def solve_ends(groups):
    count = len(groups)
    on = [g[0] >= 0.0 for g in groups]
    edges = [jnp.zeros_like(groups[0][0])]
    for i in range(1, count):
        edges.append(jnp.where(jnp.logical_and(on[i - 1], on[i]), groups[i][2], 0.0))
    leaks, srcs = [], []
    for i in range(count):
        leak, src, lo_edge = groups[i][:3]
        leak = leak + (lo_edge - edges[i])
        if i + 1 < count:
            leak = leak + (groups[i + 1][3] + (groups[i + 1][2] - edges[i + 1]))
            src = src + groups[i + 1][4]
        else:
            leak = leak + 1.0
        leaks.append(jnp.where(on[i], leak, 1.0))
        srcs.append(jnp.where(on[i], src, 0.0))
    inverse = []
    for i in range(count):
        if i + 1 < count:
            inv = 1.0 / (leaks[i] + edges[i + 1])
            share = edges[i + 1] * inv
            leaks[i + 1] = leaks[i + 1] + share * leaks[i]
            srcs[i + 1] = srcs[i + 1] + share * srcs[i]
        else:
            inv = 1.0 / leaks[i]
        inverse.append(inv)
    values = [None] * count
    values[-1] = srcs[-1] * inverse[-1]
    for i in reversed(range(count - 1)):
        values[i] = (srcs[i] + edges[i + 1] * values[i + 1]) * inverse[i]
    return values


def far_first(i, count):
    side = 1 - 2 * lax.rem(i, 2)
    return count // 2 + side * lax.div(i + 1, 2)


def sweep_kernel(
    count_x, count_y, basins,
    sol_hbm, forc_hbm, visc_hbm, blk_hbm, layers_hbm, frozen_hbm, basin_hbm,
    smooth_ref, column_ref, total_ref,
    sol_ref, forc_ref, visc_ref, blk_ref, layers_ref, frozen_ref, basin_ref,
    edge_out, edge_in, side_out, side_in, halo_out, halo_in, row_out, row_in, line_out, line_in, ends_buf,
    core_out, core_in, ring_buf, plane_buf, load_sem, send_sem, recv_sem, ready_sem,
):
    cx, cz = factors(count_x)
    rows, lanes = visc_ref.shape
    y_cells = layers_ref.shape[1]
    layers = lanes // y_cells
    chunks = lanes // LANE
    group = 2 * cz
    seg = group // 8
    gx, gy = lax.axis_index("gx"), lax.axis_index("gy")
    core = lax.rem(gx, 2)
    pz = lax.rem(lax.div(gx, 2), cz)
    px = lax.div(gx, 2 * cz)
    partner = gx + 1 - 2 * core
    seats = SEATS if group >= 24 else tuple(range(1, chunks + 1))
    member = 2 * pz + core
    place = jnp.int32(chunks)
    for i in range(chunks):
        place = jnp.where(member == seats[i], i, place)
    owning = place < chunks
    low_edge = jnp.logical_and(owning, place == 0)
    high_edge = jnp.logical_and(owning, place == 1)
    order = [0, chunks - 1] + list(range(1, chunks - 1))
    place_of = {chunk: i for i, chunk in enumerate(order)}

    def along_y(step):
        return lax.rem(gy + step + count_y, count_y)

    def gx_of(x, z, c):
        return (x * cz + z) * 2 + c

    def owner_of(place):
        return gx_of(px, seats[place] // 2, seats[place] % 2)

    loads = [
        pltpu.make_async_copy(src, dst, load_sem.at[i])
        for i, (src, dst) in enumerate((
            (layers_hbm, layers_ref), (frozen_hbm, frozen_ref), (sol_hbm, sol_ref),
            (visc_hbm, visc_ref), (blk_hbm, blk_ref), (forc_hbm, forc_ref), (basin_hbm, basin_ref),
        ))
    ]
    for copy in loads:
        copy.start()

    barrier = pltpu.get_barrier_semaphore()

    def greet(y):
        def one(i, carry):
            to = gx_of(px, cz - 1 - lax.div(i, 2), lax.rem(i, 2))

            @pl.when(jnp.logical_or(to != gx, y != gy))
            def _():
                pl.semaphore_signal(barrier, inc=1, device_id=(to, y), device_id_type=MESH)

            return carry

        return one

    @pl.when(owning)
    def _():
        lax.fori_loop(0, group, greet(gy), 0)
        for i in range(1, cx):
            pl.semaphore_signal(
                barrier, inc=1, device_id=(gx_of(lax.rem(px + i, cx), pz, core), gy),
                device_id_type=MESH,
            )

    @pl.when(low_edge)
    def _():
        lax.fori_loop(0, group, greet(along_y(-1)), 0)

    @pl.when(high_edge)
    def _():
        lax.fori_loop(0, group, greet(along_y(1)), 0)

    def remote(src, dst, k, to):
        return pltpu.make_async_remote_copy(
            src_ref=src, dst_ref=dst, send_sem=send_sem.at[k], recv_sem=recv_sem.at[k],
            device_id=to, device_id_type=MESH,
        )

    def wait_rows(sem, ref, count):
        view = ref.at[pl.ds(0, count)]
        pltpu.make_async_copy(view, view, sem).wait()

    for step in (1, -1):
        pl.semaphore_signal(barrier, inc=1, device_id=(gx, along_y(step)), device_id_type=MESH)

    lane = lax.broadcasted_iota(jnp.int32, (rows, lanes), 1)

    def cell_of(index):
        return ((index.astype(F32) + 0.5) * (1.0 / layers)).astype(jnp.int32)

    layer = lane - cell_of(lane) * layers
    wide = lax.broadcasted_iota(jnp.int32, (y_cells, lanes), 1)
    spread = jnp.where(
        cell_of(wide) == lax.broadcasted_iota(jnp.int32, (y_cells, lanes), 0), 1.0, 0.0
    ).astype(F32)
    loads[0].wait()
    loads[1].wait()
    filled = jnp.dot(layers_ref[...].astype(F32), spread, precision=HIGHEST, preferred_element_type=F32)
    frozen = jnp.dot(frozen_ref[...].astype(F32), spread, precision=HIGHEST, preferred_element_type=F32)
    active = layer.astype(F32) + 0.5 < filled
    bottom, top = layer == 0, layer == layers - 1
    slide = 1.0 - frozen

    def masked(value):
        return jnp.where(active, value, 0.0)

    loads[2].wait()
    state = [masked(sol_ref[k]) for k in range(4)]
    small = lax.broadcasted_iota(jnp.int32, (rows, LANE), 1)

    def facing_up(value):
        return jnp.where(small < layers, roll(value[:, lanes - LANE:], layers), 0.0)

    def facing_down(value):
        return jnp.where(small >= LANE - layers, roll(value[:, :LANE], LANE - layers), 0.0)

    def inner_neighbours(values):
        out = []
        for v in values:
            before = jnp.where(lane < layers, 0.0, roll(v, layers))
            after = jnp.where(lane >= lanes - layers, 0.0, roll(v, lanes - layers))
            below = jnp.where(bottom, v * slide, roll(v, 1))
            above = jnp.where(top, 0.0, roll(v, lanes - 1))
            out.append((before + after) + (below + above))
        return out

    def block(k, j):
        return blk_ref[4 * k + j]

    for k in range(3):
        edge_out[0, pl.ds(k * rows, rows)] = facing_up(state[k])
        edge_out[1, pl.ds(k * rows, rows)] = facing_down(state[k])
    around = inner_neighbours(state[:3])
    wide_rows = 2 * rows
    loads[6].wait()
    names = basin_ref[...].astype(F32)
    for side, column in ((0, y_cells - 1), (1, 0)):
        side_out[side, pl.ds(rows, rows)] = jnp.broadcast_to(names[:, column:column + 1], (rows, LANE))
    loads[3].wait()
    weight = masked(0.25 * visc_ref[...])
    side_out[0, pl.ds(0, rows)] = facing_up(weight)
    side_out[1, pl.ds(0, rows)] = facing_down(weight)
    loads[4].wait()
    loads[5].wait()
    inv_visc = 1.0 / visc_ref[...]
    for k in range(3):
        acc = forc_ref[k]
        for j in range(4):
            if j != k:
                acc = acc - block(k, j) * state[j]
        rhs = masked(acc * inv_visc + 0.25 * around[k])
        diag = jnp.where(active, block(k, k) * inv_visc, -1.0)
        for j in range(chunks):
            at = place_of[j] * 16 + k * wide_rows
            row_out[pl.ds(at, rows)] = diag[:, j * LANE:(j + 1) * LANE]
            row_out[pl.ds(at + rows, rows)] = rhs[:, j * LANE:(j + 1) * LANE]

    @pl.when(owning)
    def _():
        pl.semaphore_wait(barrier, chunks - 1 + 4 + cx - 1)

    @pl.when(jnp.logical_not(owning))
    def _():
        pl.semaphore_wait(barrier, chunks + 4)

    def to_owner(at):
        src = row_out.at[pl.ds(at * 16, 3 * wide_rows)]
        dst = row_in.at[pl.ds(pl.multiple_of(member * 16, 16), 3 * wide_rows)]

        @pl.when(place == at)
        def _():
            pltpu.make_async_copy(src, dst, recv_sem.at[4]).start()

        @pl.when(place != at)
        def _():
            remote(src, dst, 4, (owner_of(at), gy)).start()

    for side, step in ((0, 1), (1, -1)):
        remote(
            edge_out.at[side],
            edge_in.at[side, pl.ds(pl.multiple_of(member * 8, 8), 8)],
            side, (owner_of(side), along_y(step)),
        ).start()
    for at in reversed(range(chunks)):
        to_owner(at)

    sides = []
    for side, step in ((0, 1), (1, -1)):
        copy = remote(side_out.at[side], side_in.at[side], 11 + side, (gx, along_y(step)))
        copy.start()
        sides.append(copy)

    @pl.when(owning)
    def _():
        @pl.when(low_edge)
        def _():
            wait_rows(recv_sem.at[0], edge_in.at[0], group * 8)

        @pl.when(high_edge)
        def _():
            wait_rows(recv_sem.at[1], edge_in.at[1], group * 8)

        wait_rows(recv_sem.at[4], row_in, group * 3 * wide_rows)
        low_on = jnp.logical_and(low_edge, gy > 0)
        high_on = jnp.logical_and(high_edge, gy < count_y - 1)
        ways = []
        for k in range(3):
            def load(t, q, k=k):
                value = row_in[pl.ds(t * 16 + k * wide_rows + q, 8, stride=seg * 16), :]
                if q >= rows:
                    at = pl.ds(t * 8 + k * rows + q - rows, 8, stride=seg * 8)
                    low = jnp.where(low_on, edge_in[0, at, :], 0.0)
                    high = jnp.where(high_on, edge_in[1, at, :], 0.0)
                    value = value + 0.25 * (low + high)
                return value

            found, back = reduce_lines(load, seg)
            for i, value in enumerate(found):
                ends_buf[px, 3 * i + k:3 * i + k + 1] = value[7:8]
            ways.append(back)

        for i in range(cx - 1):
            x = lax.rem(px + far_first(i, cx), cx)
            remote(ends_buf.at[px], ends_buf.at[px], 10, (gx_of(x, pz, core), gy)).start()
        wait_rows(recv_sem.at[10], ends_buf, cx - 1)
        ends = solve_ends([[ends_buf[x, 3 * i:3 * i + 3] for i in range(5)] for x in range(cx)])
        own, previous = jnp.zeros((3, LANE), F32), jnp.zeros((3, LANE), F32)
        for x in range(cx):
            own = jnp.where(px == x, ends[x], own)
            previous = jnp.where(px == x + 1, ends[x], previous)
        for k in range(3):
            for t, pair in enumerate(ways[k](own[k:k + 1], previous[k:k + 1])):
                for r in range(rows):
                    line_out[pl.ds(t * 8 + k * rows + r, 8, stride=seg * 8), :] = pair[r]

        def give(i, carry):
            z = lax.rem(pz + far_first(lax.div(i, 2), cz), cz)
            m = 2 * z + lax.rem(i, 2)
            to = gx_of(px, z, lax.rem(i, 2))
            src = line_out.at[pl.ds(pl.multiple_of(m * 8, 8), 3 * rows)]
            dst = line_in.at[pl.ds(pl.multiple_of(place * 8, 8), 3 * rows)]

            @pl.when(to == gx)
            def _():
                pltpu.make_async_copy(src, dst, recv_sem.at[5]).start()

            @pl.when(to != gx)
            def _():
                remote(src, dst, 5, (to, gy)).start()

            return carry

        lax.fori_loop(0, group, give, 0)

    eye = lax.broadcasted_iota(jnp.int32, (y_cells, y_cells), 0) == lax.broadcasted_iota(
        jnp.int32, (y_cells, y_cells), 1
    )
    basin_idx = lax.broadcasted_iota(jnp.int32, (y_cells, basins), 1).astype(F32)
    belongs = []
    for x in range(rows):
        column = jnp.sum(jnp.where(eye, names[x:x + 1], 0.0), axis=1, keepdims=True)
        belongs.append(jnp.where(basin_idx == column, 1.0, 0.0).astype(F32))

    for copy in sides:
        copy.wait_recv()
    wait_rows(recv_sem.at[5], line_in, chunks * 3 * rows)
    solved = [
        jnp.concatenate([line_in[pl.ds(place_of[j] * 8 + k * rows, rows)] for j in range(chunks)], 1)
        for k in range(3)
    ]
    change = [solved[k] - state[k] for k in range(3)]

    beside = []
    for side, on in ((0, gy > 0), (1, gy < count_y - 1)):
        given = jnp.where(on, side_in[side, pl.ds(0, rows)], 0.0)
        at = (lanes - LANE) * side
        beside.append([
            jnp.sum(given * change[k][:, at:at + LANE], axis=1, keepdims=True) for k in range(3)
        ])
    halos = []
    for side, step in ((0, 1), (1, -1)):
        for k in range(3):
            halo_out[side, pl.ds(k * rows, rows)] = jnp.broadcast_to(beside[1 - side][k], (rows, LANE))
        copy = remote(halo_out.at[side], halo_in.at[side], 2 + side, (gx, along_y(step)))
        copy.start()
        halos.append(copy)

    reach = 1
    rounds = []
    while reach < count_y // 2:
        rounds.append(reach)
        reach *= 2

    def tell(k):
        for step in (rounds[k], -rounds[k]):
            pl.semaphore_signal(
                ready_sem.at[k], inc=1, device_id=(gx, along_y(step)), device_id_type=MESH
            )

    if rounds:
        tell(0)
    acc = forc_ref[3] - block(3, 3) * state[3]
    for k in range(3):
        acc = acc - block(3, k) * solved[k]
    step = masked(acc * inv_visc)
    for k in range(3):
        smooth_ref[k] = jnp.where(active, solved[k], sol_ref[k])
    smooth_ref[3] = sol_ref[3] + step
    around = inner_neighbours(change)
    coupled = []
    for k in range(3):
        acc = block(k, 3) * step
        for j in range(3):
            if j != k:
                acc = acc + block(k, j) * change[j]
        coupled.append(acc)
    post = [masked(0.25 * visc_ref[...] * around[k] - coupled[k]) for k in range(3)]
    post.append((visc_ref[...] - block(3, 3)) * step)
    by_row = jnp.concatenate([post[k][x:x + 1] for x in range(rows) for k in range(4)], 0)
    sums = lax.dot_general(
        by_row, spread, (((1,), (1,)), ((), ())), precision=HIGHEST, preferred_element_type=F32
    )
    part = jnp.dot(sums[0:4], belongs[0], precision=HIGHEST, preferred_element_type=F32)
    for x in range(1, rows):
        part = part + jnp.dot(
            sums[4 * x:4 * x + 4], belongs[x], precision=HIGHEST, preferred_element_type=F32
        )

    index4 = lax.broadcasted_iota(jnp.int32, (4, basins), 1).astype(F32)
    for side in range(2):
        for x in range(rows):
            amount = jnp.concatenate(
                [beside[side][k][x:x + 1] for k in range(3)] + [jnp.zeros((1, 1), F32)], 0
            )
            name = side_in[side, rows + x:rows + x + 1, 0:1]
            part = part + jnp.where(index4 == name, amount, 0.0)

    pieces = basins // LANE
    ring_buf[pz] = jnp.concatenate([part[:, j * LANE:(j + 1) * LANE] for j in range(pieces)], 0)

    def to_ring(i, carry):
        z = lax.rem(pz + far_first(i, cz), cz)
        remote(ring_buf.at[pz], ring_buf.at[pz], 7, (gx_of(px, z, core), gy)).start()
        return carry

    lax.fori_loop(0, cz - 1, to_ring, 0)
    if rounds:
        pl.semaphore_wait(ready_sem.at[0], 2)
        for k in range(1, len(rounds)):
            tell(k)
            if k + 1 < len(rounds):
                pl.semaphore_wait(ready_sem.at[k], 2)
    for copy in halos:
        copy.wait_recv()
    column_idx = lax.broadcasted_iota(jnp.int32, (1, y_cells), 1)
    for x in range(rows):
        for k in range(4):
            value = sums[4 * x + k:4 * x + k + 1]
            if k < 3:
                at = k * rows + x
                low, high = (halo_in[side, at:at + 1, 0:y_cells] for side in range(2))
                value = value + jnp.where(column_idx == 0, low, 0.0)
                value = value + jnp.where(column_idx == y_cells - 1, high, 0.0)
            column_ref[k, x:x + 1, :] = value
    wait_rows(recv_sem.at[7], ring_buf, cz - 1)
    own = ring_buf[0]
    for i in range(1, cz):
        own = own + ring_buf[i]
    if len(rounds) > 1:
        pl.semaphore_wait(ready_sem.at[len(rounds) - 1], 2)
    here = px * count_y + gy
    plane_buf[here] = own

    def to_plane(i, carry):
        x = lax.rem(px + far_first(lax.rem(i, cx), cx), cx)
        y = lax.rem(gy + far_first(lax.div(i, cx), count_y), count_y)
        remote(plane_buf.at[here], plane_buf.at[here], 8, (gx_of(x, pz, core), y)).start()
        return carry

    lax.fori_loop(0, cx * count_y - 1, to_plane, 0)
    wait_rows(recv_sem.at[8], plane_buf, cx * count_y - 1)
    own = plane_buf[0]
    for i in range(1, cx * count_y):
        own = own + plane_buf[i]
    core_out[...] = own
    last = remote(core_out, core_in, 9, (partner, gy))
    last.start()
    last.wait_recv()
    own = own + core_in[...]
    for j in range(pieces):
        width = min(LANE, total_ref.shape[1] - j * LANE)
        if width > 0:
            total_ref[:, j * LANE:j * LANE + width] = own[4 * j:4 * j + 4, :width]

    for copy in sides + halos + [last]:
        copy.wait_send()
    for side in range(2):
        wait_rows(send_sem.at[side], edge_out.at[side], 8)

    @pl.when(owning)
    def _():
        wait_rows(send_sem.at[4], row_out, (chunks - 1) * 3 * wide_rows)
        wait_rows(send_sem.at[5], line_out, (group - 1) * 3 * rows)
        wait_rows(send_sem.at[10], ends_buf, cx - 1)

    @pl.when(jnp.logical_not(owning))
    def _():
        wait_rows(send_sem.at[4], row_out, chunks * 3 * wide_rows)

    wait_rows(send_sem.at[7], ring_buf, cz - 1)
    wait_rows(send_sem.at[8], plane_buf, cx * count_y - 1)


def solution(mesh):
    count_x, count_y = mesh.shape["gx"], mesh.shape["gy"]
    cx, cz = factors(count_x)

    def local(sol, forc, visc, blocks, layers, frozen, basin_map):
        rows, lanes = visc.shape
        chunks = lanes // LANE
        basins = count_x // 2 * count_y
        padded = -(-basins // LANE) * LANE
        size = 4 * padded // LANE
        vmem = pl.BlockSpec(memory_space=pltpu.VMEM)
        anywhere = pl.BlockSpec(memory_space=pl.ANY)
        results = (
            jax.ShapeDtypeStruct(sol.shape, F32),
            jax.ShapeDtypeStruct((4,) + layers.shape, F32),
            jax.ShapeDtypeStruct((4, basins), F32),
        )
        inputs = (sol, forc, visc, blocks, layers, frozen, basin_map)
        return pl.pallas_call(
            functools.partial(sweep_kernel, count_x, count_y, padded),
            out_shape=results,
            in_specs=[anywhere] * 7,
            out_specs=(vmem, vmem, vmem),
            scratch_shapes=[pltpu.VMEM(a.shape, a.dtype) for a in inputs] + [
                pltpu.VMEM((2, 8, LANE), F32),
                pltpu.VMEM((2, 2 * cz * 8, LANE), F32),
                pltpu.VMEM((2, 2 * rows, LANE), F32),
                pltpu.VMEM((2, 2 * rows, LANE), F32),
                pltpu.VMEM((2, 3 * rows, LANE), F32),
                pltpu.VMEM((2, 3 * rows, LANE), F32),
                pltpu.VMEM((chunks * 16, LANE), F32),
                pltpu.VMEM((2 * cz * 16, LANE), F32),
                pltpu.VMEM((2 * cz * 8, LANE), F32),
                pltpu.VMEM((chunks * 8, LANE), F32),
                pltpu.VMEM((cx, 16, LANE), F32),
                pltpu.VMEM((size, LANE), F32),
                pltpu.VMEM((size, LANE), F32),
                pltpu.VMEM((cz, size, LANE), F32),
                pltpu.VMEM((cx * count_y, size, LANE), F32),
                pltpu.SemaphoreType.DMA((7,)),
                pltpu.SemaphoreType.DMA((13,)),
                pltpu.SemaphoreType.DMA((13,)),
                pltpu.SemaphoreType.REGULAR((4,)),
            ],
            compiler_params=pltpu.CompilerParams(
                collective_id=0, has_side_effects=True, vmem_limit_bytes=63 * 2**20
            ),
            name="sweep",
        )(*inputs)
    return jax.shard_map(
        local,
        mesh=mesh,
        in_specs=(
            P(None, "gx", "gy"), P(None, "gx", "gy"), P("gx", "gy"), P(None, "gx", "gy"),
            P("gx", "gy"), P("gx", "gy"), P("gx", "gy"),
        ),
        out_specs=(P(None, "gx", "gy"), P(None, "gx", "gy"), P()),
        check_vma=False,
    )
```

```python
import functools

import jax
import jax.numpy as jnp
from jax import lax
from jax.experimental import pallas as pl
from jax.experimental.pallas import tpu as pltpu
from jax.sharding import PartitionSpec as P

MESH = pl.DeviceIdType.MESH
HIGHEST = lax.Precision.HIGHEST
F32 = jnp.float32
LANE = 128
SEATS = (1, 2, 3, 5, 6, 8, 10, 11, 13, 15)


def factors(count_x):
    return (4, count_x // 8) if count_x == 96 else (2, count_x // 4)


def roll(value, shift, axis=1):
    size = value.shape[axis]
    return pltpu.roll(value, shift % size, axis)


def eliminate_levels(count):
    left = list(range(count))
    levels = []
    while len(left) > 1:
        gone = [pos for pos in range(0, len(left) - 1, 2)]
        levels.append([(left[p], left[p - 1] if p else None, left[p + 1]) for p in gone])
        left = [cell for pos, cell in enumerate(left) if pos not in gone]
    return levels


def reduce_lines(load, count):
    sub = lax.broadcasted_iota(jnp.int32, (8, LANE), 0)
    first, last = sub == 0, sub == 7
    one, zero = jnp.full((8, LANE), 1.0, F32), jnp.zeros((8, LANE), F32)
    d0, d1, r0, r1 = ([load(t, q) for t in range(count)] for q in range(4))
    on0 = [d >= 0.0 for d in d0]
    on1 = [d >= 0.0 for d in d1]
    r0 = [jnp.where(on, r, zero) for on, r in zip(on0, r0)]
    r1 = [jnp.where(on, r, zero) for on, r in zip(on1, r1)]
    flag1 = [jnp.where(on, one, zero) for on in on1]
    before = [jnp.where(first, one, roll(flag1[-1], 1, 0))] + flag1[:-1]
    edge_in = [jnp.where(on, b, zero) for on, b in zip(on0, before)]
    edge_mid = [jnp.where(on, f, zero) for on, f in zip(on0, flag1)]
    edge_out = edge_in[1:] + [jnp.where(last, one, roll(edge_in[0], -1, 0))]
    leak0 = [jnp.where(on, d + (2.0 - a - b), one) for on, d, a, b in zip(on0, d0, edge_in, edge_mid)]
    leak1 = [jnp.where(on, d + (2.0 - a - b), one) for on, d, a, b in zip(on1, d1, edge_mid, edge_out)]
    out_leak = jnp.where(last, roll(jnp.where(on0[0], zero, one), -1, 0), zero)
    out_src = zero
    inv0 = [1.0 / (d + (a + b)) for d, a, b in zip(leak0, edge_in, edge_mid)]
    part_leak = [d * i for d, i in zip(leak0, inv0)]
    part_src = [r * i for r, i in zip(r0, inv0)]
    give_leak = [e * p for e, p in zip(edge_in, part_leak)]
    give_src = [e * p for e, p in zip(edge_in, part_src)]
    low_leak, low_src = roll(give_leak[0], -1, 0), roll(give_src[0], -1, 0)
    out_leak, out_src = out_leak + low_leak, out_src + low_src
    give_leak = give_leak[1:] + [jnp.where(last, zero, low_leak)]
    give_src = give_src[1:] + [jnp.where(last, zero, low_src)]
    leak = [d + (e * p + g) for d, e, p, g in zip(leak1, edge_mid, part_leak, give_leak)]
    src = [r + (e * p + g) for r, e, p, g in zip(r1, edge_mid, part_src, give_src)]
    edge = [a * (b * i) for a, b, i in zip(edge_in, edge_mid, inv0)]
    kept = {}
    for level in eliminate_levels(count):
        updates = []
        for cell, low, high in level:
            lo_edge, hi_edge = edge[cell], edge[high]
            inv = 1.0 / (leak[cell] + (lo_edge + hi_edge))
            lo_share, hi_share = lo_edge * inv, hi_edge * inv
            kept[cell] = (lo_share, hi_share, src[cell] * inv)
            updates.append((cell, low, high, lo_edge * hi_share, lo_share, hi_share))
        for cell, low, high, joined, lo_share, hi_share in updates:
            low_leak, low_src = lo_share * leak[cell], lo_share * src[cell]
            if low is None:
                low_leak, low_src = roll(low_leak, -1, 0), roll(low_src, -1, 0)
                out_leak, out_src = out_leak + low_leak, out_src + low_src
                low, low_leak, low_src = count - 1, jnp.where(last, zero, low_leak), jnp.where(last, zero, low_src)
            leak[low], src[low] = leak[low] + low_leak, src[low] + low_src
            leak[high], src[high] = leak[high] + hi_share * leak[cell], src[high] + hi_share * src[cell]
            edge[high] = joined
    end_leak, end_src, lo_edge = leak[-1], src[-1], edge[-1]
    hi_edge = jnp.where(last, zero, roll(lo_edge, -1, 0))
    hops = []
    for hop in (1, 2, 4):
        gone = lax.rem(sub, 2 * hop) == hop - 1
        inv = 1.0 / jnp.where(gone, end_leak + (lo_edge + hi_edge), one)
        lo_share = jnp.where(gone, lo_edge * inv, zero)
        hi_share = jnp.where(gone, hi_edge * inv, zero)
        hops.append((hop, gone, lo_share, hi_share, end_src * inv))
        low_leak, low_src = roll(lo_share * end_leak, -hop, 0), roll(lo_share * end_src, -hop, 0)
        out_leak, out_src = out_leak + low_leak, out_src + low_src
        joined = lo_edge * hi_share
        end_leak, end_src = (
            end_leak + (jnp.where(last, zero, low_leak) + roll(hi_share * end_leak, hop, 0)),
            end_src + (jnp.where(last, zero, low_src) + roll(hi_share * end_src, hop, 0)),
        )
        lo_edge, hi_edge = roll(joined, hop, 0), jnp.where(last, zero, roll(joined, -hop, 0))
    end_leak = jnp.where(on1[-1], end_leak, -one)

    def back(own, previous):
        ends = jnp.where(last, own, zero)
        for hop, gone, lo_share, hi_share, value in reversed(hops):
            lower = jnp.where(sub < hop, previous, roll(ends, hop, 0))
            ends = jnp.where(gone, value + (lo_share * lower + hi_share * roll(ends, -hop, 0)), ends)
        value = [None] * count
        value[-1] = ends
        wrapped = jnp.where(first, previous, roll(ends, 1, 0))
        for level in reversed(eliminate_levels(count)):
            for cell, low, high in level:
                lo_share, hi_share, part = kept[cell]
                lower = wrapped if low is None else value[low]
                value[cell] = part + (lo_share * lower + hi_share * value[high])
        pairs = []
        for t in range(count):
            lower = wrapped if t == 0 else value[t - 1]
            pairs.append((part_src[t] + (edge_in[t] * lower + edge_mid[t] * value[t]) * inv0[t], value[t]))
        return pairs

    return (end_leak, end_src, lo_edge, out_leak, out_src), back


def solve_ends(groups):
    count = len(groups)
    on = [g[0] >= 0.0 for g in groups]
    edges = [jnp.zeros_like(groups[0][0])]
    for i in range(1, count):
        edges.append(jnp.where(jnp.logical_and(on[i - 1], on[i]), groups[i][2], 0.0))
    leaks, srcs = [], []
    for i in range(count):
        leak, src, lo_edge = groups[i][:3]
        leak = leak + (lo_edge - edges[i])
        if i + 1 < count:
            leak = leak + (groups[i + 1][3] + (groups[i + 1][2] - edges[i + 1]))
            src = src + groups[i + 1][4]
        else:
            leak = leak + 1.0
        leaks.append(jnp.where(on[i], leak, 1.0))
        srcs.append(jnp.where(on[i], src, 0.0))
    inverse = []
    for i in range(count):
        if i + 1 < count:
            inv = 1.0 / (leaks[i] + edges[i + 1])
            share = edges[i + 1] * inv
            leaks[i + 1] = leaks[i + 1] + share * leaks[i]
            srcs[i + 1] = srcs[i + 1] + share * srcs[i]
        else:
            inv = 1.0 / leaks[i]
        inverse.append(inv)
    values = [None] * count
    values[-1] = srcs[-1] * inverse[-1]
    for i in reversed(range(count - 1)):
        values[i] = (srcs[i] + edges[i + 1] * values[i + 1]) * inverse[i]
    return values


def far_first(i, count):
    side = 1 - 2 * lax.rem(i, 2)
    return count // 2 + side * lax.div(i + 1, 2)


def sweep_kernel(
    count_x, count_y, basins,
    sol_hbm, forc_hbm, visc_hbm, blk_hbm, layers_hbm, frozen_hbm, basin_hbm,
    smooth_ref, column_ref, total_ref,
    sol_ref, forc_ref, visc_ref, blk_ref, layers_ref, frozen_ref, basin_ref,
    edge_out, edge_in, side_out, side_in, halo_out, halo_in, row_out, row_in, line_out, line_in, ends_buf,
    core_out, core_in, ring_buf, plane_buf, load_sem, send_sem, recv_sem, ready_sem,
):
    cx, cz = factors(count_x)
    rows, lanes = visc_ref.shape
    y_cells = layers_ref.shape[1]
    layers = lanes // y_cells
    chunks = lanes // LANE
    group = 2 * cz
    seg = group // 8
    gx, gy = lax.axis_index("gx"), lax.axis_index("gy")
    core = lax.rem(gx, 2)
    pz = lax.rem(lax.div(gx, 2), cz)
    px = lax.div(gx, 2 * cz)
    partner = gx + 1 - 2 * core
    seats = SEATS if group >= 24 else tuple(range(1, chunks + 1))
    member = 2 * pz + core
    place = jnp.int32(chunks)
    for i in range(chunks):
        place = jnp.where(member == seats[i], i, place)
    owning = place < chunks
    low_edge = jnp.logical_and(owning, place == 0)
    high_edge = jnp.logical_and(owning, place == 1)
    order = [0, chunks - 1] + list(range(1, chunks - 1))
    place_of = {chunk: i for i, chunk in enumerate(order)}

    def along_y(step):
        return lax.rem(gy + step + count_y, count_y)

    def gx_of(x, z, c):
        return (x * cz + z) * 2 + c

    def owner_of(place):
        return gx_of(px, seats[place] // 2, seats[place] % 2)

    loads = [
        pltpu.make_async_copy(src, dst, load_sem.at[i])
        for i, (src, dst) in enumerate((
            (layers_hbm, layers_ref), (frozen_hbm, frozen_ref), (sol_hbm, sol_ref),
            (visc_hbm, visc_ref), (blk_hbm, blk_ref), (forc_hbm, forc_ref), (basin_hbm, basin_ref),
        ))
    ]
    for copy in loads:
        copy.start()

    barrier = pltpu.get_barrier_semaphore()

    def greet(y):
        def one(i, carry):
            to = gx_of(px, cz - 1 - lax.div(i, 2), lax.rem(i, 2))

            @pl.when(jnp.logical_or(to != gx, y != gy))
            def _():
                pl.semaphore_signal(barrier, inc=1, device_id=(to, y), device_id_type=MESH)

            return carry

        return one

    @pl.when(owning)
    def _():
        lax.fori_loop(0, group, greet(gy), 0)
        for i in range(1, cx):
            pl.semaphore_signal(
                barrier, inc=1, device_id=(gx_of(lax.rem(px + i, cx), pz, core), gy),
                device_id_type=MESH,
            )

    @pl.when(low_edge)
    def _():
        lax.fori_loop(0, group, greet(along_y(-1)), 0)

    @pl.when(high_edge)
    def _():
        lax.fori_loop(0, group, greet(along_y(1)), 0)

    def remote(src, dst, k, to):
        return pltpu.make_async_remote_copy(
            src_ref=src, dst_ref=dst, send_sem=send_sem.at[k], recv_sem=recv_sem.at[k],
            device_id=to, device_id_type=MESH,
        )

    def wait_rows(sem, ref, count):
        view = ref.at[pl.ds(0, count)]
        pltpu.make_async_copy(view, view, sem).wait()

    for step in (1, -1):
        pl.semaphore_signal(barrier, inc=1, device_id=(gx, along_y(step)), device_id_type=MESH)

    lane = lax.broadcasted_iota(jnp.int32, (rows, lanes), 1)

    def cell_of(index):
        return ((index.astype(F32) + 0.5) * (1.0 / layers)).astype(jnp.int32)

    layer = lane - cell_of(lane) * layers
    wide = lax.broadcasted_iota(jnp.int32, (y_cells, lanes), 1)
    spread = jnp.where(
        cell_of(wide) == lax.broadcasted_iota(jnp.int32, (y_cells, lanes), 0), 1.0, 0.0
    ).astype(F32)
    loads[0].wait()
    loads[1].wait()
    filled = jnp.dot(layers_ref[...].astype(F32), spread, precision=HIGHEST, preferred_element_type=F32)
    frozen = jnp.dot(frozen_ref[...].astype(F32), spread, precision=HIGHEST, preferred_element_type=F32)
    active = layer.astype(F32) + 0.5 < filled
    bottom, top = layer == 0, layer == layers - 1
    slide = 1.0 - frozen

    def masked(value):
        return jnp.where(active, value, 0.0)

    loads[2].wait()
    state = [masked(sol_ref[k]) for k in range(4)]
    small = lax.broadcasted_iota(jnp.int32, (rows, LANE), 1)

    def facing_up(value):
        return jnp.where(small < layers, roll(value[:, lanes - LANE:], layers), 0.0)

    def facing_down(value):
        return jnp.where(small >= LANE - layers, roll(value[:, :LANE], LANE - layers), 0.0)

    def inner_neighbours(values):
        out = []
        for v in values:
            before = jnp.where(lane < layers, 0.0, roll(v, layers))
            after = jnp.where(lane >= lanes - layers, 0.0, roll(v, lanes - layers))
            below = jnp.where(bottom, v * slide, roll(v, 1))
            above = jnp.where(top, 0.0, roll(v, lanes - 1))
            out.append((before + after) + (below + above))
        return out

    def block(k, j):
        return blk_ref[4 * k + j]

    for k in range(3):
        edge_out[0, pl.ds(k * rows, rows)] = facing_up(state[k])
        edge_out[1, pl.ds(k * rows, rows)] = facing_down(state[k])
    around = inner_neighbours(state[:3])
    wide_rows = 2 * rows
    loads[6].wait()
    names = basin_ref[...].astype(F32)
    for side, column in ((0, y_cells - 1), (1, 0)):
        side_out[side, pl.ds(rows, rows)] = jnp.broadcast_to(names[:, column:column + 1], (rows, LANE))
    loads[3].wait()
    weight = masked(0.25 * visc_ref[...])
    side_out[0, pl.ds(0, rows)] = facing_up(weight)
    side_out[1, pl.ds(0, rows)] = facing_down(weight)
    loads[4].wait()
    loads[5].wait()
    inv_visc = 1.0 / visc_ref[...]
    for k in range(3):
        acc = forc_ref[k]
        for j in range(4):
            if j != k:
                acc = acc - block(k, j) * state[j]
        rhs = masked(acc * inv_visc + 0.25 * around[k])
        diag = jnp.where(active, block(k, k) * inv_visc, -1.0)
        for j in range(chunks):
            at = place_of[j] * 16 + k * wide_rows
            row_out[pl.ds(at, rows)] = diag[:, j * LANE:(j + 1) * LANE]
            row_out[pl.ds(at + rows, rows)] = rhs[:, j * LANE:(j + 1) * LANE]

    @pl.when(owning)
    def _():
        pl.semaphore_wait(barrier, chunks - 1 + 4 + cx - 1)

    @pl.when(jnp.logical_not(owning))
    def _():
        pl.semaphore_wait(barrier, chunks + 4)

    def to_owner(at):
        src = row_out.at[pl.ds(at * 16, 3 * wide_rows)]
        dst = row_in.at[pl.ds(pl.multiple_of(member * 16, 16), 3 * wide_rows)]

        @pl.when(place == at)
        def _():
            pltpu.make_async_copy(src, dst, recv_sem.at[4]).start()

        @pl.when(place != at)
        def _():
            remote(src, dst, 4, (owner_of(at), gy)).start()

    for side, step in ((0, 1), (1, -1)):
        remote(
            edge_out.at[side],
            edge_in.at[side, pl.ds(pl.multiple_of(member * 8, 8), 8)],
            side, (owner_of(side), along_y(step)),
        ).start()
    for at in reversed(range(chunks)):
        to_owner(at)

    sides = []
    for side, step in ((0, 1), (1, -1)):
        copy = remote(side_out.at[side], side_in.at[side], 11 + side, (gx, along_y(step)))
        copy.start()
        sides.append(copy)

    @pl.when(owning)
    def _():
        @pl.when(low_edge)
        def _():
            wait_rows(recv_sem.at[0], edge_in.at[0], group * 8)

        @pl.when(high_edge)
        def _():
            wait_rows(recv_sem.at[1], edge_in.at[1], group * 8)

        wait_rows(recv_sem.at[4], row_in, group * 3 * wide_rows)
        low_on = jnp.logical_and(low_edge, gy > 0)
        high_on = jnp.logical_and(high_edge, gy < count_y - 1)
        ways = []
        for k in range(3):
            def load(t, q, k=k):
                value = row_in[pl.ds(t * 16 + k * wide_rows + q, 8, stride=seg * 16), :]
                if q >= rows:
                    at = pl.ds(t * 8 + k * rows + q - rows, 8, stride=seg * 8)
                    low = jnp.where(low_on, edge_in[0, at, :], 0.0)
                    high = jnp.where(high_on, edge_in[1, at, :], 0.0)
                    value = value + 0.25 * (low + high)
                return value

            found, back = reduce_lines(load, seg)
            for i, value in enumerate(found):
                ends_buf[px, 3 * i + k:3 * i + k + 1] = value[7:8]
            ways.append(back)

        for i in range(cx - 1):
            x = lax.rem(px + far_first(i, cx), cx)
            remote(ends_buf.at[px], ends_buf.at[px], 10, (gx_of(x, pz, core), gy)).start()
        wait_rows(recv_sem.at[10], ends_buf, cx - 1)
        ends = solve_ends([[ends_buf[x, 3 * i:3 * i + 3] for i in range(5)] for x in range(cx)])
        own, previous = jnp.zeros((3, LANE), F32), jnp.zeros((3, LANE), F32)
        for x in range(cx):
            own = jnp.where(px == x, ends[x], own)
            previous = jnp.where(px == x + 1, ends[x], previous)
        for k in range(3):
            for t, pair in enumerate(ways[k](own[k:k + 1], previous[k:k + 1])):
                for r in range(rows):
                    line_out[pl.ds(t * 8 + k * rows + r, 8, stride=seg * 8), :] = pair[r]

        def give(i, carry):
            z = lax.rem(pz + far_first(lax.div(i, 2), cz), cz)
            m = 2 * z + lax.rem(i, 2)
            to = gx_of(px, z, lax.rem(i, 2))
            src = line_out.at[pl.ds(pl.multiple_of(m * 8, 8), 3 * rows)]
            dst = line_in.at[pl.ds(pl.multiple_of(place * 8, 8), 3 * rows)]

            @pl.when(to == gx)
            def _():
                pltpu.make_async_copy(src, dst, recv_sem.at[5]).start()

            @pl.when(to != gx)
            def _():
                remote(src, dst, 5, (to, gy)).start()

            return carry

        lax.fori_loop(0, group, give, 0)

    eye = lax.broadcasted_iota(jnp.int32, (y_cells, y_cells), 0) == lax.broadcasted_iota(
        jnp.int32, (y_cells, y_cells), 1
    )
    basin_idx = lax.broadcasted_iota(jnp.int32, (y_cells, basins), 1).astype(F32)
    belongs = []
    for x in range(rows):
        column = jnp.sum(jnp.where(eye, names[x:x + 1], 0.0), axis=1, keepdims=True)
        belongs.append(jnp.where(basin_idx == column, 1.0, 0.0).astype(F32))

    for copy in sides:
        copy.wait_recv()
    wait_rows(recv_sem.at[5], line_in, chunks * 3 * rows)
    solved = [
        jnp.concatenate([line_in[pl.ds(place_of[j] * 8 + k * rows, rows)] for j in range(chunks)], 1)
        for k in range(3)
    ]
    change = [solved[k] - state[k] for k in range(3)]

    beside = []
    for side, on in ((0, gy > 0), (1, gy < count_y - 1)):
        given = jnp.where(on, side_in[side, pl.ds(0, rows)], 0.0)
        at = (lanes - LANE) * side
        beside.append([
            jnp.sum(given * change[k][:, at:at + LANE], axis=1, keepdims=True) for k in range(3)
        ])
    halos = []
    for side, step in ((0, 1), (1, -1)):
        for k in range(3):
            halo_out[side, pl.ds(k * rows, rows)] = jnp.broadcast_to(beside[1 - side][k], (rows, LANE))
        copy = remote(halo_out.at[side], halo_in.at[side], 2 + side, (gx, along_y(step)))
        copy.start()
        halos.append(copy)

    reach = 1
    rounds = []
    while reach < count_y // 2:
        rounds.append(reach)
        reach *= 2

    def tell(k):
        for step in (rounds[k], -rounds[k]):
            pl.semaphore_signal(
                ready_sem.at[k], inc=1, device_id=(gx, along_y(step)), device_id_type=MESH
            )

    if rounds:
        tell(0)
    acc = forc_ref[3] - block(3, 3) * state[3]
    for k in range(3):
        acc = acc - block(3, k) * solved[k]
    step = masked(acc * inv_visc)
    for k in range(3):
        smooth_ref[k] = jnp.where(active, solved[k], sol_ref[k])
    smooth_ref[3] = sol_ref[3] + step
    around = inner_neighbours(change)
    coupled = []
    for k in range(3):
        acc = block(k, 3) * step
        for j in range(3):
            if j != k:
                acc = acc + block(k, j) * change[j]
        coupled.append(acc)
    post = [masked(0.25 * visc_ref[...] * around[k] - coupled[k]) for k in range(3)]
    post.append((visc_ref[...] - block(3, 3)) * step)
    by_row = jnp.concatenate([post[k][x:x + 1] for x in range(rows) for k in range(4)], 0)
    sums = lax.dot_general(
        by_row, spread, (((1,), (1,)), ((), ())), precision=HIGHEST, preferred_element_type=F32
    )
    part = jnp.dot(sums[0:4], belongs[0], precision=HIGHEST, preferred_element_type=F32)
    for x in range(1, rows):
        part = part + jnp.dot(
            sums[4 * x:4 * x + 4], belongs[x], precision=HIGHEST, preferred_element_type=F32
        )

    index4 = lax.broadcasted_iota(jnp.int32, (4, basins), 1).astype(F32)
    for side in range(2):
        for x in range(rows):
            amount = jnp.concatenate(
                [beside[side][k][x:x + 1] for k in range(3)] + [jnp.zeros((1, 1), F32)], 0
            )
            name = side_in[side, rows + x:rows + x + 1, 0:1]
            part = part + jnp.where(index4 == name, amount, 0.0)

    pieces = basins // LANE
    ring_buf[pz] = jnp.concatenate([part[:, j * LANE:(j + 1) * LANE] for j in range(pieces)], 0)

    def to_ring(i, carry):
        z = lax.rem(pz + far_first(i, cz), cz)
        remote(ring_buf.at[pz], ring_buf.at[pz], 7, (gx_of(px, z, core), gy)).start()
        return carry

    lax.fori_loop(0, cz - 1, to_ring, 0)
    if rounds:
        pl.semaphore_wait(ready_sem.at[0], 2)
        for k in range(1, len(rounds)):
            tell(k)
            if k + 1 < len(rounds):
                pl.semaphore_wait(ready_sem.at[k], 2)
    for copy in halos:
        copy.wait_recv()
    column_idx = lax.broadcasted_iota(jnp.int32, (1, y_cells), 1)
    for x in range(rows):
        for k in range(4):
            value = sums[4 * x + k:4 * x + k + 1]
            if k < 3:
                at = k * rows + x
                low, high = (halo_in[side, at:at + 1, 0:y_cells] for side in range(2))
                value = value + jnp.where(column_idx == 0, low, 0.0)
                value = value + jnp.where(column_idx == y_cells - 1, high, 0.0)
            column_ref[k, x:x + 1, :] = value
    wait_rows(recv_sem.at[7], ring_buf, cz - 1)
    own = ring_buf[0]
    for i in range(1, cz):
        own = own + ring_buf[i]
    if len(rounds) > 1:
        pl.semaphore_wait(ready_sem.at[len(rounds) - 1], 2)
    here = px * count_y + gy
    plane_buf[here] = own

    def to_plane(i, carry):
        x = lax.rem(px + far_first(lax.rem(i, cx), cx), cx)
        y = lax.rem(gy + far_first(lax.div(i, cx), count_y), count_y)
        remote(plane_buf.at[here], plane_buf.at[here], 8, (gx_of(x, pz, core), y)).start()
        return carry

    lax.fori_loop(0, cx * count_y - 1, to_plane, 0)
    wait_rows(recv_sem.at[8], plane_buf, cx * count_y - 1)
    own = plane_buf[0]
    for i in range(1, cx * count_y):
        own = own + plane_buf[i]
    core_out[...] = own
    last = remote(core_out, core_in, 9, (partner, gy))
    last.start()
    last.wait_recv()
    own = own + core_in[...]
    for j in range(pieces):
        width = min(LANE, total_ref.shape[1] - j * LANE)
        if width > 0:
            total_ref[:, j * LANE:j * LANE + width] = own[4 * j:4 * j + 4, :width]

    for copy in sides + halos + [last]:
        copy.wait_send()
    for side in range(2):
        wait_rows(send_sem.at[side], edge_out.at[side], 8)

    @pl.when(owning)
    def _():
        wait_rows(send_sem.at[4], row_out, (chunks - 1) * 3 * wide_rows)
        wait_rows(send_sem.at[5], line_out, (group - 1) * 3 * rows)
        wait_rows(send_sem.at[10], ends_buf, cx - 1)

    @pl.when(jnp.logical_not(owning))
    def _():
        wait_rows(send_sem.at[4], row_out, chunks * 3 * wide_rows)

    wait_rows(send_sem.at[7], ring_buf, cz - 1)
    wait_rows(send_sem.at[8], plane_buf, cx * count_y - 1)


def place_kernel(*refs):
    half = (len(refs) - 1) // 2
    copies = [
        pltpu.make_async_copy(src, dst, refs[-1].at[i])
        for i, (src, dst) in enumerate(zip(refs[:half], refs[half:-1]))
    ]
    for copy in copies:
        copy.start()
    for copy in copies:
        copy.wait()


def solution(mesh):
    count_x, count_y = mesh.shape["gx"], mesh.shape["gy"]
    cx, cz = factors(count_x)

    def local(sol, forc, visc, blocks, layers, frozen, basin_map):
        rows, lanes = visc.shape
        chunks = lanes // LANE
        basins = count_x // 2 * count_y
        padded = -(-basins // LANE) * LANE
        size = 4 * padded // LANE
        vmem = pl.BlockSpec(memory_space=pltpu.VMEM)
        anywhere = pl.BlockSpec(memory_space=pl.ANY)
        results = (
            jax.ShapeDtypeStruct(sol.shape, F32),
            jax.ShapeDtypeStruct((4,) + layers.shape, F32),
            jax.ShapeDtypeStruct((4, basins), F32),
        )
        inputs = tuple(
            pltpu.with_memory_space_constraint(a, pltpu.HBM)
            for a in (sol, forc, visc, blocks, layers, frozen, basin_map)
        )
        found = pl.pallas_call(
            functools.partial(sweep_kernel, count_x, count_y, padded),
            out_shape=results,
            in_specs=[anywhere] * 7,
            out_specs=(vmem, vmem, vmem),
            scratch_shapes=[pltpu.VMEM(a.shape, a.dtype) for a in inputs] + [
                pltpu.VMEM((2, 8, LANE), F32),
                pltpu.VMEM((2, 2 * cz * 8, LANE), F32),
                pltpu.VMEM((2, 2 * rows, LANE), F32),
                pltpu.VMEM((2, 2 * rows, LANE), F32),
                pltpu.VMEM((2, 3 * rows, LANE), F32),
                pltpu.VMEM((2, 3 * rows, LANE), F32),
                pltpu.VMEM((chunks * 16, LANE), F32),
                pltpu.VMEM((2 * cz * 16, LANE), F32),
                pltpu.VMEM((2 * cz * 8, LANE), F32),
                pltpu.VMEM((chunks * 8, LANE), F32),
                pltpu.VMEM((cx, 16, LANE), F32),
                pltpu.VMEM((size, LANE), F32),
                pltpu.VMEM((size, LANE), F32),
                pltpu.VMEM((cz, size, LANE), F32),
                pltpu.VMEM((cx * count_y, size, LANE), F32),
                pltpu.SemaphoreType.DMA((7,)),
                pltpu.SemaphoreType.DMA((13,)),
                pltpu.SemaphoreType.DMA((13,)),
                pltpu.SemaphoreType.REGULAR((4,)),
            ],
            compiler_params=pltpu.CompilerParams(
                collective_id=0, has_side_effects=True, vmem_limit_bytes=32 * 2**20
            ),
            name="sweep",
        )(*inputs)
        return pl.pallas_call(
            place_kernel,
            out_shape=results,
            in_specs=[pl.BlockSpec(memory_space=pl.ANY)] * 3,
            out_specs=(pl.BlockSpec(memory_space=pl.ANY),) * 3,
            scratch_shapes=[pltpu.SemaphoreType.DMA((3,))],
            name="place",
        )(*[pltpu.with_memory_space_constraint(a, pltpu.VMEM) for a in found])
    return jax.shard_map(
        local,
        mesh=mesh,
        in_specs=(
            P(None, "gx", "gy"), P(None, "gx", "gy"), P("gx", "gy"), P(None, "gx", "gy"),
            P("gx", "gy"), P("gx", "gy"), P("gx", "gy"),
        ),
        out_specs=(P(None, "gx", "gy"), P(None, "gx", "gy"), P()),
        check_vma=False,
    )
```

```python
import functools

import jax
import jax.numpy as jnp
from jax import lax
from jax.experimental import pallas as pl
from jax.experimental.pallas import tpu as pltpu
from jax.sharding import PartitionSpec as P

MESH = pl.DeviceIdType.MESH
HIGHEST = lax.Precision.HIGHEST
F32 = jnp.float32
LANE = 128
SEATS = (1, 2, 3, 5, 6, 8, 10, 11, 13, 15)


def factors(count_x):
    return (4, count_x // 8) if count_x == 96 else (2, count_x // 4)


def roll(value, shift, axis=1):
    size = value.shape[axis]
    return pltpu.roll(value, shift % size, axis)


def eliminate_levels(count):
    left = list(range(count))
    levels = []
    while len(left) > 1:
        gone = [pos for pos in range(0, len(left) - 1, 2)]
        levels.append([(left[p], left[p - 1] if p else None, left[p + 1]) for p in gone])
        left = [cell for pos, cell in enumerate(left) if pos not in gone]
    return levels


def reduce_lines(load, count):
    sub = lax.broadcasted_iota(jnp.int32, (8, LANE), 0)
    first, last = sub == 0, sub == 7
    one, zero = jnp.full((8, LANE), 1.0, F32), jnp.zeros((8, LANE), F32)
    d0, d1, r0, r1 = ([load(t, q) for t in range(count)] for q in range(4))
    on0 = [d >= 0.0 for d in d0]
    on1 = [d >= 0.0 for d in d1]
    r0 = [jnp.where(on, r, zero) for on, r in zip(on0, r0)]
    r1 = [jnp.where(on, r, zero) for on, r in zip(on1, r1)]
    flag1 = [jnp.where(on, one, zero) for on in on1]
    before = [jnp.where(first, one, roll(flag1[-1], 1, 0))] + flag1[:-1]
    edge_in = [jnp.where(on, b, zero) for on, b in zip(on0, before)]
    edge_mid = [jnp.where(on, f, zero) for on, f in zip(on0, flag1)]
    edge_out = edge_in[1:] + [jnp.where(last, one, roll(edge_in[0], -1, 0))]
    leak0 = [jnp.where(on, d + (2.0 - a - b), one) for on, d, a, b in zip(on0, d0, edge_in, edge_mid)]
    leak1 = [jnp.where(on, d + (2.0 - a - b), one) for on, d, a, b in zip(on1, d1, edge_mid, edge_out)]
    out_leak = jnp.where(last, roll(jnp.where(on0[0], zero, one), -1, 0), zero)
    out_src = zero
    inv0 = [1.0 / (d + (a + b)) for d, a, b in zip(leak0, edge_in, edge_mid)]
    part_leak = [d * i for d, i in zip(leak0, inv0)]
    part_src = [r * i for r, i in zip(r0, inv0)]
    give_leak = [e * p for e, p in zip(edge_in, part_leak)]
    give_src = [e * p for e, p in zip(edge_in, part_src)]
    low_leak, low_src = roll(give_leak[0], -1, 0), roll(give_src[0], -1, 0)
    out_leak, out_src = out_leak + low_leak, out_src + low_src
    give_leak = give_leak[1:] + [jnp.where(last, zero, low_leak)]
    give_src = give_src[1:] + [jnp.where(last, zero, low_src)]
    leak = [d + (e * p + g) for d, e, p, g in zip(leak1, edge_mid, part_leak, give_leak)]
    src = [r + (e * p + g) for r, e, p, g in zip(r1, edge_mid, part_src, give_src)]
    edge = [a * (b * i) for a, b, i in zip(edge_in, edge_mid, inv0)]
    kept = {}
    for level in eliminate_levels(count):
        updates = []
        for cell, low, high in level:
            lo_edge, hi_edge = edge[cell], edge[high]
            inv = 1.0 / (leak[cell] + (lo_edge + hi_edge))
            lo_share, hi_share = lo_edge * inv, hi_edge * inv
            kept[cell] = (lo_share, hi_share, src[cell] * inv)
            updates.append((cell, low, high, lo_edge * hi_share, lo_share, hi_share))
        for cell, low, high, joined, lo_share, hi_share in updates:
            low_leak, low_src = lo_share * leak[cell], lo_share * src[cell]
            if low is None:
                low_leak, low_src = roll(low_leak, -1, 0), roll(low_src, -1, 0)
                out_leak, out_src = out_leak + low_leak, out_src + low_src
                low, low_leak, low_src = count - 1, jnp.where(last, zero, low_leak), jnp.where(last, zero, low_src)
            leak[low], src[low] = leak[low] + low_leak, src[low] + low_src
            leak[high], src[high] = leak[high] + hi_share * leak[cell], src[high] + hi_share * src[cell]
            edge[high] = joined
    end_leak, end_src, lo_edge = leak[-1], src[-1], edge[-1]
    hi_edge = jnp.where(last, zero, roll(lo_edge, -1, 0))
    hops = []
    for hop in (1, 2, 4):
        gone = lax.rem(sub, 2 * hop) == hop - 1
        inv = 1.0 / jnp.where(gone, end_leak + (lo_edge + hi_edge), one)
        lo_share = jnp.where(gone, lo_edge * inv, zero)
        hi_share = jnp.where(gone, hi_edge * inv, zero)
        hops.append((hop, gone, lo_share, hi_share, end_src * inv))
        low_leak, low_src = roll(lo_share * end_leak, -hop, 0), roll(lo_share * end_src, -hop, 0)
        out_leak, out_src = out_leak + low_leak, out_src + low_src
        joined = lo_edge * hi_share
        end_leak, end_src = (
            end_leak + (jnp.where(last, zero, low_leak) + roll(hi_share * end_leak, hop, 0)),
            end_src + (jnp.where(last, zero, low_src) + roll(hi_share * end_src, hop, 0)),
        )
        lo_edge, hi_edge = roll(joined, hop, 0), jnp.where(last, zero, roll(joined, -hop, 0))
    end_leak = jnp.where(on1[-1], end_leak, -one)

    def back(own, previous):
        ends = jnp.where(last, own, zero)
        for hop, gone, lo_share, hi_share, value in reversed(hops):
            lower = jnp.where(sub < hop, previous, roll(ends, hop, 0))
            ends = jnp.where(gone, value + (lo_share * lower + hi_share * roll(ends, -hop, 0)), ends)
        value = [None] * count
        value[-1] = ends
        wrapped = jnp.where(first, previous, roll(ends, 1, 0))
        for level in reversed(eliminate_levels(count)):
            for cell, low, high in level:
                lo_share, hi_share, part = kept[cell]
                lower = wrapped if low is None else value[low]
                value[cell] = part + (lo_share * lower + hi_share * value[high])
        pairs = []
        for t in range(count):
            lower = wrapped if t == 0 else value[t - 1]
            pairs.append((part_src[t] + (edge_in[t] * lower + edge_mid[t] * value[t]) * inv0[t], value[t]))
        return pairs

    return (end_leak, end_src, lo_edge, out_leak, out_src), back


def solve_ends(groups):
    count = len(groups)
    on = [g[0] >= 0.0 for g in groups]
    edges = [jnp.zeros_like(groups[0][0])]
    for i in range(1, count):
        edges.append(jnp.where(jnp.logical_and(on[i - 1], on[i]), groups[i][2], 0.0))
    leaks, srcs = [], []
    for i in range(count):
        leak, src, lo_edge = groups[i][:3]
        leak = leak + (lo_edge - edges[i])
        if i + 1 < count:
            leak = leak + (groups[i + 1][3] + (groups[i + 1][2] - edges[i + 1]))
            src = src + groups[i + 1][4]
        else:
            leak = leak + 1.0
        leaks.append(jnp.where(on[i], leak, 1.0))
        srcs.append(jnp.where(on[i], src, 0.0))
    inverse = []
    for i in range(count):
        if i + 1 < count:
            inv = 1.0 / (leaks[i] + edges[i + 1])
            share = edges[i + 1] * inv
            leaks[i + 1] = leaks[i + 1] + share * leaks[i]
            srcs[i + 1] = srcs[i + 1] + share * srcs[i]
        else:
            inv = 1.0 / leaks[i]
        inverse.append(inv)
    values = [None] * count
    values[-1] = srcs[-1] * inverse[-1]
    for i in reversed(range(count - 1)):
        values[i] = (srcs[i] + edges[i + 1] * values[i + 1]) * inverse[i]
    return values


def far_first(i, count):
    side = 1 - 2 * lax.rem(i, 2)
    return count // 2 + side * lax.div(i + 1, 2)


def sweep_kernel(
    count_x, count_y, basins,
    sol_hbm, forc_hbm, visc_hbm, blk_hbm, layers_hbm, frozen_hbm, basin_hbm,
    smooth_ref, column_ref, total_ref,
    sol_ref, forc_ref, visc_ref, blk_ref, layers_ref, frozen_ref, basin_ref,
    edge_out, edge_in, side_out, side_in, halo_out, halo_in, row_out, row_in, line_out, line_in, ends_buf,
    core_out, core_in, ring_buf, plane_buf, load_sem, send_sem, recv_sem, ready_sem,
):
    cx, cz = factors(count_x)
    rows, lanes = visc_ref.shape
    y_cells = layers_ref.shape[1]
    layers = lanes // y_cells
    chunks = lanes // LANE
    group = 2 * cz
    seg = group // 8
    gx, gy = lax.axis_index("gx"), lax.axis_index("gy")
    core = lax.rem(gx, 2)
    pz = lax.rem(lax.div(gx, 2), cz)
    px = lax.div(gx, 2 * cz)
    partner = gx + 1 - 2 * core
    seats = SEATS if group >= 24 else tuple(range(1, chunks + 1))
    member = 2 * pz + core
    place = jnp.int32(chunks)
    for i in range(chunks):
        place = jnp.where(member == seats[i], i, place)
    owning = place < chunks
    low_edge = jnp.logical_and(owning, place == 0)
    high_edge = jnp.logical_and(owning, place == 1)
    order = [0, chunks - 1] + list(range(1, chunks - 1))
    place_of = {chunk: i for i, chunk in enumerate(order)}

    def along_y(step):
        return lax.rem(gy + step + count_y, count_y)

    def gx_of(x, z, c):
        return (x * cz + z) * 2 + c

    def owner_of(place):
        return gx_of(px, seats[place] // 2, seats[place] % 2)

    loads = [
        pltpu.make_async_copy(src, dst, load_sem.at[i])
        for i, (src, dst) in enumerate((
            (layers_hbm, layers_ref), (frozen_hbm, frozen_ref), (sol_hbm, sol_ref),
            (visc_hbm, visc_ref), (blk_hbm.at[pl.ds(0, 12)], blk_ref.at[pl.ds(0, 12)]),
            (forc_hbm, forc_ref), (basin_hbm, basin_ref),
            (blk_hbm.at[pl.ds(12, 4)], blk_ref.at[pl.ds(12, 4)]),
        ))
    ]
    for i in (4, 5, 2, 3, 0, 1, 6, 7):
        loads[i].start()

    barrier = pltpu.get_barrier_semaphore()

    def greet(y):
        def one(i, carry):
            to = gx_of(px, cz - 1 - lax.div(i, 2), lax.rem(i, 2))

            @pl.when(jnp.logical_or(to != gx, y != gy))
            def _():
                pl.semaphore_signal(barrier, inc=1, device_id=(to, y), device_id_type=MESH)

            return carry

        return one

    @pl.when(owning)
    def _():
        lax.fori_loop(0, group, greet(gy), 0)
        for i in range(1, cx):
            pl.semaphore_signal(
                barrier, inc=1, device_id=(gx_of(lax.rem(px + i, cx), pz, core), gy),
                device_id_type=MESH,
            )

    @pl.when(low_edge)
    def _():
        lax.fori_loop(0, group, greet(along_y(-1)), 0)

    @pl.when(high_edge)
    def _():
        lax.fori_loop(0, group, greet(along_y(1)), 0)

    def remote(src, dst, k, to):
        return pltpu.make_async_remote_copy(
            src_ref=src, dst_ref=dst, send_sem=send_sem.at[k], recv_sem=recv_sem.at[k],
            device_id=to, device_id_type=MESH,
        )

    def wait_rows(sem, ref, count):
        view = ref.at[pl.ds(0, count)]
        pltpu.make_async_copy(view, view, sem).wait()

    for step in (1, -1):
        pl.semaphore_signal(barrier, inc=1, device_id=(gx, along_y(step)), device_id_type=MESH)

    lane = lax.broadcasted_iota(jnp.int32, (rows, lanes), 1)

    def cell_of(index):
        return ((index.astype(F32) + 0.5) * (1.0 / layers)).astype(jnp.int32)

    layer = lane - cell_of(lane) * layers
    wide = lax.broadcasted_iota(jnp.int32, (y_cells, lanes), 1)
    spread = jnp.where(
        cell_of(wide) == lax.broadcasted_iota(jnp.int32, (y_cells, lanes), 0), 1.0, 0.0
    ).astype(F32)
    loads[0].wait()
    loads[1].wait()
    filled = jnp.dot(layers_ref[...].astype(F32), spread, precision=HIGHEST, preferred_element_type=F32)
    frozen = jnp.dot(frozen_ref[...].astype(F32), spread, precision=HIGHEST, preferred_element_type=F32)
    active = layer.astype(F32) + 0.5 < filled
    bottom, top = layer == 0, layer == layers - 1
    slide = 1.0 - frozen

    def masked(value):
        return jnp.where(active, value, 0.0)

    loads[2].wait()
    state = [masked(sol_ref[k]) for k in range(4)]
    small = lax.broadcasted_iota(jnp.int32, (rows, LANE), 1)

    def facing_up(value):
        return jnp.where(small < layers, roll(value[:, lanes - LANE:], layers), 0.0)

    def facing_down(value):
        return jnp.where(small >= LANE - layers, roll(value[:, :LANE], LANE - layers), 0.0)

    def inner_neighbours(values):
        out = []
        for v in values:
            before = jnp.where(lane < layers, 0.0, roll(v, layers))
            after = jnp.where(lane >= lanes - layers, 0.0, roll(v, lanes - layers))
            below = jnp.where(bottom, v * slide, roll(v, 1))
            above = jnp.where(top, 0.0, roll(v, lanes - 1))
            out.append((before + after) + (below + above))
        return out

    def block(k, j):
        return blk_ref[4 * k + j]

    for k in range(3):
        edge_out[0, pl.ds(k * rows, rows)] = facing_up(state[k])
        edge_out[1, pl.ds(k * rows, rows)] = facing_down(state[k])
    around = inner_neighbours(state[:3])
    wide_rows = 2 * rows
    loads[6].wait()
    names = basin_ref[...].astype(F32)
    for side, column in ((0, y_cells - 1), (1, 0)):
        side_out[side, pl.ds(rows, rows)] = jnp.broadcast_to(names[:, column:column + 1], (rows, LANE))
    loads[3].wait()
    weight = masked(0.25 * visc_ref[...])
    side_out[0, pl.ds(0, rows)] = facing_up(weight)
    side_out[1, pl.ds(0, rows)] = facing_down(weight)
    loads[4].wait()
    loads[5].wait()
    inv_visc = 1.0 / visc_ref[...]
    for k in range(3):
        acc = forc_ref[k]
        for j in range(4):
            if j != k:
                acc = acc - block(k, j) * state[j]
        rhs = masked(acc * inv_visc + 0.25 * around[k])
        diag = jnp.where(active, block(k, k) * inv_visc, -1.0)
        for j in range(chunks):
            at = place_of[j] * 16 + k * wide_rows
            row_out[pl.ds(at, rows)] = diag[:, j * LANE:(j + 1) * LANE]
            row_out[pl.ds(at + rows, rows)] = rhs[:, j * LANE:(j + 1) * LANE]

    @pl.when(owning)
    def _():
        pl.semaphore_wait(barrier, chunks - 1 + 4 + cx - 1)

    @pl.when(jnp.logical_not(owning))
    def _():
        pl.semaphore_wait(barrier, chunks + 4)

    def to_owner(at):
        src = row_out.at[pl.ds(at * 16, 3 * wide_rows)]
        dst = row_in.at[pl.ds(pl.multiple_of(member * 16, 16), 3 * wide_rows)]

        @pl.when(place == at)
        def _():
            pltpu.make_async_copy(src, dst, recv_sem.at[4]).start()

        @pl.when(place != at)
        def _():
            remote(src, dst, 4, (owner_of(at), gy)).start()

    for side, step in ((0, 1), (1, -1)):
        remote(
            edge_out.at[side],
            edge_in.at[side, pl.ds(pl.multiple_of(member * 8, 8), 8)],
            side, (owner_of(side), along_y(step)),
        ).start()
    for at in reversed(range(chunks)):
        to_owner(at)

    sides = []
    for side, step in ((0, 1), (1, -1)):
        copy = remote(side_out.at[side], side_in.at[side], 11 + side, (gx, along_y(step)))
        copy.start()
        sides.append(copy)

    @pl.when(owning)
    def _():
        @pl.when(low_edge)
        def _():
            wait_rows(recv_sem.at[0], edge_in.at[0], group * 8)

        @pl.when(high_edge)
        def _():
            wait_rows(recv_sem.at[1], edge_in.at[1], group * 8)

        wait_rows(recv_sem.at[4], row_in, group * 3 * wide_rows)
        low_on = jnp.logical_and(low_edge, gy > 0)
        high_on = jnp.logical_and(high_edge, gy < count_y - 1)
        ways = []
        for k in range(3):
            def load(t, q, k=k):
                value = row_in[pl.ds(t * 16 + k * wide_rows + q, 8, stride=seg * 16), :]
                if q >= rows:
                    at = pl.ds(t * 8 + k * rows + q - rows, 8, stride=seg * 8)
                    low = jnp.where(low_on, edge_in[0, at, :], 0.0)
                    high = jnp.where(high_on, edge_in[1, at, :], 0.0)
                    value = value + 0.25 * (low + high)
                return value

            found, back = reduce_lines(load, seg)
            for i, value in enumerate(found):
                ends_buf[px, 3 * i + k:3 * i + k + 1] = value[7:8]
            ways.append(back)

        for i in range(cx - 1):
            x = lax.rem(px + far_first(i, cx), cx)
            remote(ends_buf.at[px], ends_buf.at[px], 10, (gx_of(x, pz, core), gy)).start()
        wait_rows(recv_sem.at[10], ends_buf, cx - 1)
        ends = solve_ends([[ends_buf[x, 3 * i:3 * i + 3] for i in range(5)] for x in range(cx)])
        own, previous = jnp.zeros((3, LANE), F32), jnp.zeros((3, LANE), F32)
        for x in range(cx):
            own = jnp.where(px == x, ends[x], own)
            previous = jnp.where(px == x + 1, ends[x], previous)
        for k in range(3):
            for t, pair in enumerate(ways[k](own[k:k + 1], previous[k:k + 1])):
                for r in range(rows):
                    line_out[pl.ds(t * 8 + k * rows + r, 8, stride=seg * 8), :] = pair[r]

        def give(i, carry):
            z = lax.rem(pz + far_first(lax.div(i, 2), cz), cz)
            m = 2 * z + lax.rem(i, 2)
            to = gx_of(px, z, lax.rem(i, 2))
            src = line_out.at[pl.ds(pl.multiple_of(m * 8, 8), 3 * rows)]
            dst = line_in.at[pl.ds(pl.multiple_of(place * 8, 8), 3 * rows)]

            @pl.when(to == gx)
            def _():
                pltpu.make_async_copy(src, dst, recv_sem.at[5]).start()

            @pl.when(to != gx)
            def _():
                remote(src, dst, 5, (to, gy)).start()

            return carry

        lax.fori_loop(0, group, give, 0)

    loads[7].wait()
    eye = lax.broadcasted_iota(jnp.int32, (y_cells, y_cells), 0) == lax.broadcasted_iota(
        jnp.int32, (y_cells, y_cells), 1
    )
    basin_idx = lax.broadcasted_iota(jnp.int32, (y_cells, basins), 1).astype(F32)
    belongs = []
    for x in range(rows):
        column = jnp.sum(jnp.where(eye, names[x:x + 1], 0.0), axis=1, keepdims=True)
        belongs.append(jnp.where(basin_idx == column, 1.0, 0.0).astype(F32))

    for copy in sides:
        copy.wait_recv()
    wait_rows(recv_sem.at[5], line_in, chunks * 3 * rows)
    solved = [
        jnp.concatenate([line_in[pl.ds(place_of[j] * 8 + k * rows, rows)] for j in range(chunks)], 1)
        for k in range(3)
    ]
    change = [solved[k] - state[k] for k in range(3)]

    beside = []
    for side, on in ((0, gy > 0), (1, gy < count_y - 1)):
        given = jnp.where(on, side_in[side, pl.ds(0, rows)], 0.0)
        at = (lanes - LANE) * side
        beside.append([
            jnp.sum(given * change[k][:, at:at + LANE], axis=1, keepdims=True) for k in range(3)
        ])
    halos = []
    for side, step in ((0, 1), (1, -1)):
        for k in range(3):
            halo_out[side, pl.ds(k * rows, rows)] = jnp.broadcast_to(beside[1 - side][k], (rows, LANE))
        copy = remote(halo_out.at[side], halo_in.at[side], 2 + side, (gx, along_y(step)))
        copy.start()
        halos.append(copy)

    reach = 1
    rounds = []
    while reach < count_y // 2:
        rounds.append(reach)
        reach *= 2

    def tell(k):
        for step in (rounds[k], -rounds[k]):
            pl.semaphore_signal(
                ready_sem.at[k], inc=1, device_id=(gx, along_y(step)), device_id_type=MESH
            )

    if rounds:
        tell(0)
    acc = forc_ref[3] - block(3, 3) * state[3]
    for k in range(3):
        acc = acc - block(3, k) * solved[k]
    step = masked(acc * inv_visc)
    for k in range(3):
        smooth_ref[k] = jnp.where(active, solved[k], sol_ref[k])
    smooth_ref[3] = sol_ref[3] + step
    around = inner_neighbours(change)
    coupled = []
    for k in range(3):
        acc = block(k, 3) * step
        for j in range(3):
            if j != k:
                acc = acc + block(k, j) * change[j]
        coupled.append(acc)
    post = [masked(0.25 * visc_ref[...] * around[k] - coupled[k]) for k in range(3)]
    post.append((visc_ref[...] - block(3, 3)) * step)
    by_row = jnp.concatenate([post[k][x:x + 1] for x in range(rows) for k in range(4)], 0)
    sums = lax.dot_general(
        by_row, spread, (((1,), (1,)), ((), ())), precision=HIGHEST, preferred_element_type=F32
    )
    part = jnp.dot(sums[0:4], belongs[0], precision=HIGHEST, preferred_element_type=F32)
    for x in range(1, rows):
        part = part + jnp.dot(
            sums[4 * x:4 * x + 4], belongs[x], precision=HIGHEST, preferred_element_type=F32
        )

    index4 = lax.broadcasted_iota(jnp.int32, (4, basins), 1).astype(F32)
    for side in range(2):
        for x in range(rows):
            amount = jnp.concatenate(
                [beside[side][k][x:x + 1] for k in range(3)] + [jnp.zeros((1, 1), F32)], 0
            )
            name = side_in[side, rows + x:rows + x + 1, 0:1]
            part = part + jnp.where(index4 == name, amount, 0.0)

    pieces = basins // LANE
    ring_buf[pz] = jnp.concatenate([part[:, j * LANE:(j + 1) * LANE] for j in range(pieces)], 0)

    def to_ring(i, carry):
        z = lax.rem(pz + far_first(i, cz), cz)
        remote(ring_buf.at[pz], ring_buf.at[pz], 7, (gx_of(px, z, core), gy)).start()
        return carry

    lax.fori_loop(0, cz - 1, to_ring, 0)
    if rounds:
        pl.semaphore_wait(ready_sem.at[0], 2)
        for k in range(1, len(rounds)):
            tell(k)
            if k + 1 < len(rounds):
                pl.semaphore_wait(ready_sem.at[k], 2)
    for copy in halos:
        copy.wait_recv()
    column_idx = lax.broadcasted_iota(jnp.int32, (1, y_cells), 1)
    for x in range(rows):
        for k in range(4):
            value = sums[4 * x + k:4 * x + k + 1]
            if k < 3:
                at = k * rows + x
                low, high = (halo_in[side, at:at + 1, 0:y_cells] for side in range(2))
                value = value + jnp.where(column_idx == 0, low, 0.0)
                value = value + jnp.where(column_idx == y_cells - 1, high, 0.0)
            column_ref[k, x:x + 1, :] = value
    wait_rows(recv_sem.at[7], ring_buf, cz - 1)
    own = ring_buf[0]
    for i in range(1, cz):
        own = own + ring_buf[i]
    if len(rounds) > 1:
        pl.semaphore_wait(ready_sem.at[len(rounds) - 1], 2)
    here = px * count_y + gy
    plane_buf[here] = own

    def to_plane(i, carry):
        x = lax.rem(px + far_first(lax.rem(i, cx), cx), cx)
        y = lax.rem(gy + far_first(lax.div(i, cx), count_y), count_y)
        remote(plane_buf.at[here], plane_buf.at[here], 8, (gx_of(x, pz, core), y)).start()
        return carry

    lax.fori_loop(0, cx * count_y - 1, to_plane, 0)
    wait_rows(recv_sem.at[8], plane_buf, cx * count_y - 1)
    own = plane_buf[0]
    for i in range(1, cx * count_y):
        own = own + plane_buf[i]
    core_out[...] = own
    last = remote(core_out, core_in, 9, (partner, gy))
    last.start()
    last.wait_recv()
    own = own + core_in[...]
    for j in range(pieces):
        width = min(LANE, total_ref.shape[1] - j * LANE)
        if width > 0:
            total_ref[:, j * LANE:j * LANE + width] = own[4 * j:4 * j + 4, :width]

    for copy in sides + halos + [last]:
        copy.wait_send()
    for side in range(2):
        wait_rows(send_sem.at[side], edge_out.at[side], 8)

    @pl.when(owning)
    def _():
        wait_rows(send_sem.at[4], row_out, (chunks - 1) * 3 * wide_rows)
        wait_rows(send_sem.at[5], line_out, (group - 1) * 3 * rows)
        wait_rows(send_sem.at[10], ends_buf, cx - 1)

    @pl.when(jnp.logical_not(owning))
    def _():
        wait_rows(send_sem.at[4], row_out, chunks * 3 * wide_rows)

    wait_rows(send_sem.at[7], ring_buf, cz - 1)
    wait_rows(send_sem.at[8], plane_buf, cx * count_y - 1)


def place_kernel(*refs):
    half = (len(refs) - 1) // 2
    copies = [
        pltpu.make_async_copy(src, dst, refs[-1].at[i])
        for i, (src, dst) in enumerate(zip(refs[:half], refs[half:-1]))
    ]
    for copy in copies:
        copy.start()
    for copy in copies:
        copy.wait()


def solution(mesh):
    count_x, count_y = mesh.shape["gx"], mesh.shape["gy"]
    cx, cz = factors(count_x)

    def local(sol, forc, visc, blocks, layers, frozen, basin_map):
        rows, lanes = visc.shape
        chunks = lanes // LANE
        basins = count_x // 2 * count_y
        padded = -(-basins // LANE) * LANE
        size = 4 * padded // LANE
        vmem = pl.BlockSpec(memory_space=pltpu.VMEM)
        anywhere = pl.BlockSpec(memory_space=pl.ANY)
        results = (
            jax.ShapeDtypeStruct(sol.shape, F32),
            jax.ShapeDtypeStruct((4,) + layers.shape, F32),
            jax.ShapeDtypeStruct((4, basins), F32),
        )
        inputs = tuple(
            pltpu.with_memory_space_constraint(a, pltpu.HBM)
            for a in (sol, forc, visc, blocks, layers, frozen, basin_map)
        )
        found = pl.pallas_call(
            functools.partial(sweep_kernel, count_x, count_y, padded),
            out_shape=results,
            in_specs=[anywhere] * 7,
            out_specs=(vmem, vmem, vmem),
            scratch_shapes=[pltpu.VMEM(a.shape, a.dtype) for a in inputs] + [
                pltpu.VMEM((2, 8, LANE), F32),
                pltpu.VMEM((2, 2 * cz * 8, LANE), F32),
                pltpu.VMEM((2, 2 * rows, LANE), F32),
                pltpu.VMEM((2, 2 * rows, LANE), F32),
                pltpu.VMEM((2, 3 * rows, LANE), F32),
                pltpu.VMEM((2, 3 * rows, LANE), F32),
                pltpu.VMEM((chunks * 16, LANE), F32),
                pltpu.VMEM((2 * cz * 16, LANE), F32),
                pltpu.VMEM((2 * cz * 8, LANE), F32),
                pltpu.VMEM((chunks * 8, LANE), F32),
                pltpu.VMEM((cx, 16, LANE), F32),
                pltpu.VMEM((size, LANE), F32),
                pltpu.VMEM((size, LANE), F32),
                pltpu.VMEM((cz, size, LANE), F32),
                pltpu.VMEM((cx * count_y, size, LANE), F32),
                pltpu.SemaphoreType.DMA((8,)),
                pltpu.SemaphoreType.DMA((13,)),
                pltpu.SemaphoreType.DMA((13,)),
                pltpu.SemaphoreType.REGULAR((4,)),
            ],
            compiler_params=pltpu.CompilerParams(
                collective_id=0, has_side_effects=True, vmem_limit_bytes=32 * 2**20
            ),
            name="sweep",
        )(*inputs)
        return pl.pallas_call(
            place_kernel,
            out_shape=results,
            in_specs=[pl.BlockSpec(memory_space=pl.ANY)] * 3,
            out_specs=(pl.BlockSpec(memory_space=pl.ANY),) * 3,
            scratch_shapes=[pltpu.SemaphoreType.DMA((3,))],
            name="place",
        )(*[pltpu.with_memory_space_constraint(a, pltpu.VMEM) for a in found])
    return jax.shard_map(
        local,
        mesh=mesh,
        in_specs=(
            P(None, "gx", "gy"), P(None, "gx", "gy"), P("gx", "gy"), P(None, "gx", "gy"),
            P("gx", "gy"), P("gx", "gy"), P("gx", "gy"),
        ),
        out_specs=(P(None, "gx", "gy"), P(None, "gx", "gy"), P()),
        check_vma=False,
    )
```
